32 devices in a mesh: sec: 8 (over z, x), op: 4 (over y, core).
Axes of the slice: x: 2, y: 2, z: 4, core: 2. Of those that a mesh axis runs over, the one named last changes fastest.
Arguments:
- state: float32 [8, 256, 256], P('sec'), may hold values from -6 to 6
- left_ops: float32 [32, 8, 256, 256], P('op', 'sec'), may hold values from -0.0625 to 0.0625
- right_ops: float32 [32, 8, 256, 256], P('op', 'sec'), may hold values from -0.375 to 0.375
- term_shift: int32 [32], P('op'), may hold values from -1 to 1
- sector_rows: int32 [8], P('sec'), may hold values from 128 to 256, as said below
- sector_cols: int32 [8], P('sec'), may hold values from 128 to 256, as said below
Outputs:
- correction: float32 [8, 256, 256], P('sec')
- image: float32 [8, 256, 256], P('sec')
The draws below stay inside these ranges and needn't reach their ends.
Inputs may be any that keep to these rules, and one draw needn't show every extreme that they name: `sector_rows`: at least one sector has 256 live rows. `sector_cols`: at least one sector has 256 live columns.
All inputs are finite; a program needn't handle non-finite values.
Results may differ from the reference program's by a relative error of at most 0.0003.
Values sent between devices are 32-bit elements; how exact they have to be, the bound alone decides.
No kernel may reach another device: no remote copies, remote signals or barrier semaphores. Data moves between devices by JAX's collectives and lax.ppermute only.
A program may use at most 64 MiB of HBM per device.

```python
import jax
import jax.numpy as jnp
from jax import lax

BLOCK = 256
SECTORS = 8
TERMS = 32


def live_counts(key):
    values = jax.random.randint(key, (SECTORS,), BLOCK // 2, BLOCK + 1)
    where_full = jax.random.randint(jax.random.fold_in(key, 7), (), 0, SECTORS)
    place = jnp.arange(SECTORS, dtype=jnp.int32)
    return jnp.where(place == where_full, BLOCK, values).astype(jnp.int32)


def draw_sector_rows(key, part):
    return live_counts(jax.random.fold_in(key, 11))


def draw_sector_cols(key, part):
    return live_counts(jax.random.fold_in(key, 23))


def with_ends(values, own_key, low, high):
    spot = [jax.random.randint(jax.random.fold_in(own_key, axis), (), 0, length) for axis, length in enumerate(values.shape)]
    longest = values.shape.index(max(values.shape))
    next_to = spot[:longest] + [(spot[longest] + 1) % values.shape[longest]] + spot[longest + 1:]
    return values.at[tuple(spot)].set(low).at[tuple(next_to)].set(high)


def level_of(stream_key, extent, shards, smallest, largest):
    def one(axis_at, blocks):
        draws = jax.random.uniform(jax.random.fold_in(jax.random.fold_in(stream_key, 6), axis_at), (blocks,), jnp.float32, smallest / len(shards), largest / len(shards))
        return jnp.repeat(jnp.exp(draws), extent[axis_at] // blocks).reshape((-1,) + (1,) * (len(extent) - axis_at - 1))

    gain = one(*shards[0])
    for cut in shards[1:]:
        gain = gain * one(*cut)
    return gain


def bell_draw(key, shape, deviation, reach, cuts=(), kind=jnp.bfloat16):
    values = deviation * jax.random.normal(key, shape, jnp.float32)
    if cuts:
        values = values * level_of(key, shape, cuts, -0.22, 0.18)
    return jnp.clip(values, -reach, reach).astype(kind)


def setup_inputs(seed: int = 0) -> dict:
    streams_of = jax.random.split(jax.random.key(seed), 7)
    return {
        "state": bell_draw(streams_of[0], (SECTORS, BLOCK, BLOCK), 1.0, 6.0, ((0, 8),), jnp.float32),
        "left_ops": bell_draw(streams_of[1], (TERMS, SECTORS, BLOCK, BLOCK), (BLOCK * TERMS) ** -0.5, 0.0625, ((0, 4), (1, 8)), jnp.float32),
        "right_ops": bell_draw(streams_of[2], (TERMS, SECTORS, BLOCK, BLOCK), BLOCK ** -0.5, 0.375, ((0, 4), (1, 8)), jnp.float32),
        "term_shift": with_ends(jax.random.randint(streams_of[3], (TERMS,), -1, 2), jax.random.fold_in(streams_of[3], 1), -1, 1).astype(jnp.int32),
        "sector_rows": draw_sector_rows(jax.random.fold_in(streams_of[6], 71), 0),
        "sector_cols": draw_sector_cols(jax.random.fold_in(streams_of[6], 71), 0),
    }


def live_mask(sector_rows, sector_cols, block):
    place = jnp.arange(block, dtype=jnp.int32)
    rows_ok = place[None, :, None] < sector_rows[:, None, None]
    cols_ok = place[None, None, :] < sector_cols[:, None, None]
    return (rows_ok & cols_ok).astype(jnp.float32)

def hamiltonian(field, left_ops, right_ops, term_shift, mask):
    count = field.shape[0]
    padded = jnp.pad(field, ((1, 1), (0, 0), (0, 0)))

    def step(total, items):
        left, right, shift = items
        source = lax.dynamic_slice_in_dim(padded, (1 - shift).astype(jnp.int32), count, 0)
        inner = jnp.einsum('tij,tjl->til', left, source, precision=lax.Precision.HIGHEST)
        total = total + jnp.einsum('til,tml->tim', inner, right, precision=lax.Precision.HIGHEST)
        return (total, None)
    total, _ = lax.scan(step, jnp.zeros(field.shape, jnp.float32), (left_ops, right_ops, term_shift))
    return total * mask

def reference(state, left_ops, right_ops, term_shift, sector_rows, sector_cols):
    mask = live_mask(sector_rows, sector_cols, BLOCK)
    field = state * mask
    first = hamiltonian(field, left_ops, right_ops, term_shift, mask)
    theta = jnp.sum(field * first) / jnp.sum(field * field)
    resid = first - theta * field
    scale = lax.rsqrt(jnp.sum(resid * resid) / (SECTORS * BLOCK * BLOCK) + 1e-06)
    correction = resid * scale
    image = hamiltonian(correction, left_ops, right_ops, term_shift, mask)
    return (correction, image)
```

```python
import jax
import jax.numpy as jnp
from jax import lax
from jax.experimental import pallas as pl
from jax.experimental.pallas import tpu as pltpu
from jax.sharding import PartitionSpec as P

EXTRA = 8


def split(x):
    high = x.astype(jnp.bfloat16)
    low = (x - high.astype(jnp.float32)).astype(jnp.bfloat16)
    return high, low


def dot(a, b, contract):
    return lax.dot_general(
        a, b, (((1,), (contract,)), ((), ())), preferred_element_type=jnp.float32
    )


def product_kernel(place_ref, shift_ref, own_ref, near_ref, far_ref, left_ref, right_ref, *refs):
    core, slot = place_ref[0], place_ref[1]
    extra_ref = refs[0] if len(refs) == 6 else None
    send_ref, keep_ref, high, low, total = refs[-5:]
    for index, ref in ((1, own_ref), (slot, near_ref), (2 - slot, far_ref)):
        high[index], low[index] = split(ref[...])
    out = None
    for term in range(left_ref.shape[0]):
        source = 1 - shift_ref[term]
        left_high, left_low = split(left_ref[term, 0])
        right_high, right_low = split(right_ref[term, 0])
        v_high, v_low = high[source], low[source]
        inner = dot(left_high, v_high, 0) + (dot(left_low, v_high, 0) + dot(left_high, v_low, 0))
        inner_high, inner_low = split(inner)
        part = dot(inner_high, right_high, 1) + (
            dot(inner_low, right_high, 1) + dot(inner_high, right_low, 1)
        )
        out = part if out is None else out + part
    total[...] = out
    half = out.shape[0] // 2
    send_ref[pl.ds(0, half)] = total[pl.ds(pl.multiple_of((1 - core) * half, half), half)]
    keep_ref[pl.ds(0, half)] = total[pl.ds(pl.multiple_of(core * half, half), half)]
    if extra_ref is not None:
        send_ref[pl.ds(half, EXTRA)] = extra_ref[...]
        keep_ref[pl.ds(half, EXTRA)] = extra_ref[...]


def product(place, shift, own, near, far, left_ops, right_ops, extra=None):
    block = own.shape[0]
    rows = block // 2 + (0 if extra is None else EXTRA)
    vmem, smem = pl.BlockSpec(memory_space=pltpu.VMEM), pl.BlockSpec(memory_space=pltpu.SMEM)
    arrays = [own, near, far, left_ops, right_ops] + ([] if extra is None else [extra])
    return pl.pallas_call(
        product_kernel,
        out_shape=[jax.ShapeDtypeStruct((rows, own.shape[1]), jnp.float32)] * 2,
        in_specs=[smem, smem] + [vmem] * len(arrays),
        out_specs=[vmem, vmem],
        scratch_shapes=[
            pltpu.VMEM((3,) + own.shape, jnp.bfloat16),
            pltpu.VMEM((3,) + own.shape, jnp.bfloat16),
            pltpu.VMEM(own.shape, jnp.float32),
        ],
        compiler_params=pltpu.CompilerParams(vmem_limit_bytes=24 * 1024 * 1024),
        cost_estimate=pl.CostEstimate(
            flops=12 * left_ops.shape[0] * block**3, bytes_accessed=8 * left_ops.size, transcendentals=0
        ),
    )(place, shift, *arrays)


def live_mask(sector_rows, sector_cols, block):
    place = jnp.arange(block, dtype=jnp.int32)
    rows_ok = place[:, None] < sector_rows[0]
    cols_ok = place[None, :] < sector_cols[0]
    return (rows_ok & cols_ok).astype(jnp.float32)


def local(state, left_ops, right_ops, term_shift, sector_rows, sector_cols):
    sectors, ops = lax.axis_size("sec"), lax.axis_size("op")
    block = state.shape[1]
    half = block // 2
    cells = sectors * block * block
    sector, op = lax.axis_index("sec"), lax.axis_index("op")
    core = op % 2

    others = [(i, i ^ 1) for i in range(ops)]
    even = [(i, i + 1) for i in range(0, sectors - 1, 2)]
    odd = [(i, i + 1) for i in range(1, sectors - 1, 2)]
    neighbours = []
    for a in range(ops):
        for one, two in (even, odd)[a % 2]:
            neighbours += [(one * ops + a, two * ops + a), (two * ops + a, one * ops + a)]
    slot = jnp.where(sector % 2 == core, 2, 0)
    place = jnp.stack([core, slot]).astype(jnp.int32)

    mask = live_mask(sector_rows, sector_cols, block)
    field = state[0] * mask

    def exchange(v):
        near = lax.ppermute(v, ("sec", "op"), neighbours)
        return near, lax.ppermute(near, "op", others)

    def halves_summed(send, keep):
        total = keep + lax.ppermute(send, "op", others)
        step = 2
        while step < ops:
            total = total + lax.ppermute(total, "op", [(i, i ^ step) for i in range(ops)])
            step *= 2
        return total

    def joined(mine):
        other = lax.ppermute(mine, "op", others)
        return jnp.where(
            core == 0, jnp.concatenate([mine, other]), jnp.concatenate([other, mine])
        )

    def half_of(v):
        return jnp.where(core == 0, v[:half], v[half:])

    near, far = exchange(field)
    send, keep = product(place, term_shift, field, near, far, left_ops, right_ops)
    first = joined(halves_summed(send, keep) * half_of(mask))
    near, far = exchange(first)

    cross, square = jnp.sum(field * first), jnp.sum(field * field)
    own_theta = jnp.where(square > 0, cross / jnp.where(square > 0, square, 1.0), 0.0)
    own_resid = first - own_theta * field
    energy = jnp.sum(own_resid * own_resid)
    row = lax.broadcasted_iota(jnp.int32, (EXTRA, block), 0)
    lane = lax.broadcasted_iota(jnp.int32, (EXTRA, block), 1)
    values = jnp.where(row == 0, cross, jnp.where(row == 1, square, jnp.where(row == 2, energy, 0.0)))
    mine = jnp.where(lane == sector, values, 0.0)
    sums = jnp.where(op == 0, mine, 0.0)
    for base in range(1, sectors, ops):
        pairs = [
            (s * ops + a, (s + base + a) % sectors * ops + a)
            for s in range(sectors)
            for a in range(ops)
            if base + a < sectors
        ]
        sums = sums + lax.ppermute(mine, ("sec", "op"), pairs)

    send, keep = product(place, term_shift, first, near, far, left_ops, right_ops, sums)
    total = halves_summed(send, keep)
    crosses, squares, energies = (total[half + i, :] for i in range(3))
    theta = jnp.sum(crosses) / jnp.sum(squares)
    thetas = jnp.where(squares > 0, crosses / jnp.where(squares > 0, squares, 1.0), 0.0)
    energy = jnp.sum(energies + (thetas - theta) ** 2 * squares)
    scale = lax.rsqrt(energy / cells + 1e-06)
    image = joined(scale * (total[:half] - theta * half_of(first)) * half_of(mask))
    correction = scale * (first - theta * field)
    return correction[None], image[None]


def solution(mesh):
    in_specs = (
        P("sec", None, None),
        P("op", "sec", None, None),
        P("op", "sec", None, None),
        P("op"),
        P("sec"),
        P("sec"),
    )
    out_specs = (P("sec", None, None), P("sec", None, None))
    return jax.shard_map(local, mesh=mesh, in_specs=in_specs, out_specs=out_specs, check_vma=False)
```

```python
import jax
import jax.numpy as jnp
from jax import lax
from jax.experimental import pallas as pl
from jax.experimental.pallas import tpu as pltpu
from jax.sharding import PartitionSpec as P

EXTRA = 8
VMEM = pl.BlockSpec(memory_space=pltpu.VMEM)
HBM = pl.BlockSpec(memory_space=pltpu.HBM)


def f32(*shape):
    return jax.ShapeDtypeStruct(shape, jnp.float32)


def in_hbm(x):
    return pltpu.with_memory_space_constraint(x, pltpu.HBM)


def call(kernel, out_shape, in_specs, *arrays, mib=4, **options):
    return pl.pallas_call(
        kernel,
        out_shape=out_shape,
        in_specs=in_specs,
        out_specs=jax.tree.map(lambda _: VMEM, out_shape),
        compiler_params=pltpu.CompilerParams(vmem_limit_bytes=mib * 1024 * 1024),
        **options,
    )(*arrays)


def core_index():
    return lax.rem(lax.axis_index("op"), 2)


def rows_of(core, half):
    return pl.ds(pl.multiple_of(core * half, half), half)


def split(x):
    high = x.astype(jnp.bfloat16)
    low = (x - high.astype(jnp.float32)).astype(jnp.bfloat16)
    return high, low


def dot(a, b, contract):
    return lax.dot_general(
        a, b, (((1,), (contract,)), ((), ())), preferred_element_type=jnp.float32
    )


def total_of(x):
    return jnp.sum(jnp.sum(x, axis=0, keepdims=True), axis=1, keepdims=True)


def field_kernel(state_ref, live_ref, mine_ref, other_ref, mask_ref, state, live, sems):
    copies = [
        pltpu.make_async_copy(ref, buffer, sems.at[i])
        for i, (ref, buffer) in enumerate(
            ((state_ref, state), (live_ref, live))
        )
    ]
    for copy in copies:
        copy.start()
    for copy in copies:
        copy.wait()
    half = mask_ref.shape[0]
    core = core_index()
    rows, cols = live[0], live[1]
    row = lax.broadcasted_iota(jnp.int32, mask_ref.shape, 0)
    lane = lax.broadcasted_iota(jnp.int32, mask_ref.shape, 1)
    for which, ref in ((core, mine_ref), (1 - core, other_ref)):
        inside = (row + which * half < rows) & (lane < cols)
        ref[...] = jnp.where(inside, state[0, rows_of(which, half)], 0.0)
    mask_ref[...] = jnp.where((row + core * half < rows) & (lane < cols), 1.0, 0.0)


def load_kernel(left_ref, right_ref, field_ref, left_out, right_out, sems):
    copies = [
        pltpu.make_async_copy(left_ref, left_out, sems.at[0]),
        pltpu.make_async_copy(right_ref, right_out, sems.at[1]),
    ]
    for copy in copies:
        copy.start()
    for copy in copies:
        copy.wait()


def load(left_ops, right_ops, field):
    return call(
        load_kernel,
        [f32(*left_ops.shape), f32(*right_ops.shape)],
        [HBM, HBM, VMEM],
        in_hbm(left_ops), in_hbm(right_ops), field,
        scratch_shapes=[pltpu.SemaphoreType.DMA((2,))],
        cost_estimate=pl.CostEstimate(flops=0, bytes_accessed=8 * left_ops.size, transcendentals=0),
    )


def product_kernel(shift_ref, *refs):
    halves, (left_ref, right_ref) = refs[:6], refs[6:8]
    tile_ref = refs[8] if len(refs) == 16 else None
    send_ref, keep_ref, high, low, total, shift, sem = refs[-7:]
    shifts = pltpu.make_async_copy(shift_ref, shift, sem)
    shifts.start()
    block = total.shape[0]
    half = block // 2
    core, sector = core_index(), lax.axis_index("sec")
    slot = jnp.where(lax.rem(sector, 2) == 0, 2, 0)
    for index, mine_ref, other_ref in zip((1, slot, 2 - slot), halves[::2], halves[1::2]):
        for which, ref in ((core, mine_ref), (1 - core, other_ref)):
            rows = rows_of(which, half)
            high[index, rows], low[index, rows] = split(ref[...])

    @pl.when(sector == 0)
    def _():
        high[0] = jnp.zeros(high.shape[1:], high.dtype)
        low[0] = jnp.zeros(low.shape[1:], low.dtype)

    @pl.when(sector == lax.axis_size("sec") - 1)
    def _():
        high[2] = jnp.zeros(high.shape[1:], high.dtype)
        low[2] = jnp.zeros(low.shape[1:], low.dtype)

    shifts.wait()
    out = None
    for term in range(left_ref.shape[0]):
        source = 1 - shift[term]
        left_high, left_low = split(left_ref[term, 0])
        right_high, right_low = split(right_ref[term, 0])
        v_high, v_low = high[source], low[source]
        inner = dot(left_high, v_high, 0) + (dot(left_low, v_high, 0) + dot(left_high, v_low, 0))
        inner_high, inner_low = split(inner)
        part = dot(inner_high, right_high, 1) + (
            dot(inner_low, right_high, 1) + dot(inner_high, right_low, 1)
        )
        out = part if out is None else out + part
    total[...] = out
    send_ref[pl.ds(0, half)] = total[rows_of(1 - core, half)]
    keep_ref[pl.ds(0, half)] = total[rows_of(core, half)]
    if tile_ref is not None:
        send_ref[pl.ds(half, EXTRA)] = tile_ref[...]
        keep_ref[pl.ds(half, EXTRA)] = tile_ref[...]


def product(shift, halves, left, right, tile=None):
    terms, _, block, _ = left.shape
    rows = block // 2 + (0 if tile is None else EXTRA)
    arrays = [*halves, left, right] + ([] if tile is None else [tile])
    return call(
        product_kernel,
        [f32(rows, block)] * 2,
        [HBM] + [VMEM] * len(arrays),
        in_hbm(shift), *arrays,
        mib=16,
        scratch_shapes=[
            pltpu.VMEM((3, block, block), jnp.bfloat16),
            pltpu.VMEM((3, block, block), jnp.bfloat16),
            pltpu.VMEM((block, block), jnp.float32),
            pltpu.SMEM(shift.shape, jnp.int32),
            pltpu.SemaphoreType.DMA(()),
        ],
        cost_estimate=pl.CostEstimate(
            flops=12 * terms * block**3, bytes_accessed=4 * left.size, transcendentals=0
        ),
    )


def tile_kernel(first_ref, first_other_ref, field_ref, field_other_ref, out_ref):
    first = jnp.concatenate([first_ref[...], first_other_ref[...]])
    field = jnp.concatenate([field_ref[...], field_other_ref[...]])
    cross, square = total_of(field * first), total_of(field * field)
    theta = jnp.where(square > 0, cross / jnp.where(square > 0, square, 1.0), 0.0)
    resid = first - theta * field
    energy = total_of(resid * resid)
    row = lax.broadcasted_iota(jnp.int32, out_ref.shape, 0)
    lane = lax.broadcasted_iota(jnp.int32, out_ref.shape, 1)
    values = jnp.where(row == 0, cross, jnp.where(row == 1, square, jnp.where(row == 2, energy, 0.0)))
    out_ref[...] = jnp.where(lane == lax.axis_index("sec"), values, 0.0)


def gathered_kernel(ops, sectors, tile_ref, *refs):
    *tile_refs, out_ref = refs
    op = lax.axis_index("op")
    total = jnp.where(op == 0, tile_ref[...], 0.0)
    for i, ref in enumerate(tile_refs):
        total = total + jnp.where(1 + i * ops + op < sectors, ref[...], 0.0)
    out_ref[...] = total


def merged(sums, cells):
    crosses, squares, energies = (sums[i : i + 1] for i in range(3))
    theta = jnp.sum(crosses, axis=1, keepdims=True) / jnp.sum(squares, axis=1, keepdims=True)
    thetas = jnp.where(squares > 0, crosses / jnp.where(squares > 0, squares, 1.0), 0.0)
    energy = jnp.sum(energies + (thetas - theta) ** 2 * squares, axis=1, keepdims=True)
    return theta, lax.rsqrt(energy / cells + 1e-06)


def image_kernel(cells, total_ref, peer_ref, mask_ref, first_ref, out_ref):
    half = out_ref.shape[0]
    theta, scale = merged(total_ref[pl.ds(half, EXTRA)] + peer_ref[pl.ds(half, EXTRA)], cells)
    total = (total_ref[pl.ds(0, half)] + peer_ref[pl.ds(0, half)]) * mask_ref[...]
    out_ref[...] = scale * (total - theta * first_ref[...])


def correction_kernel(cells, total_ref, peer_ref, first_ref, first_other_ref, field_ref, field_other_ref, out_ref):
    half = first_ref.shape[0]
    core = core_index()
    tile = pl.ds(half, EXTRA)
    theta, scale = merged(total_ref[tile] + peer_ref[tile], cells)
    out_ref[0, rows_of(core, half)] = scale * (first_ref[...] - theta * field_ref[...])
    out_ref[0, rows_of(1 - core, half)] = scale * (first_other_ref[...] - theta * field_other_ref[...])


def output_kernel(mine_ref, other_ref, out_ref):
    half = mine_ref.shape[0]
    core = core_index()
    out_ref[0, rows_of(core, half)] = mine_ref[...]
    out_ref[0, rows_of(1 - core, half)] = other_ref[...]


def local(state, left_ops, right_ops, term_shift, sector_rows, sector_cols):
    sectors, ops = lax.axis_size("sec"), lax.axis_size("op")
    block = state.shape[1]
    half = block // 2

    others = [(i, i ^ 1) for i in range(ops)]
    pairs = [(s, s ^ 1) for s in range(sectors)]
    between = []
    for a in range(ops):
        between += [(s * ops + a, s * ops + (a ^ 2)) for s in (0, sectors - 1)]
        for s in range(1, sectors - 1, 2):
            between += [(s * ops + a, (s + 1) * ops + a), ((s + 1) * ops + a, s * ops + a)]

    def swapped(v):
        return lax.ppermute(v, "op", others)

    def neighbours(mine):
        return lax.ppermute(mine, ("sec", "op"), between), lax.ppermute(mine, "sec", pairs)

    def over_chips(send, keep):
        total = keep + swapped(send)
        step = 2
        while step < ops // 2:
            total = total + lax.ppermute(total, "op", [(i, i ^ step) for i in range(ops)])
            step *= 2
        return total, lax.ppermute(total, "op", [(i, i ^ step) for i in range(ops)])

    field, field_other, mask = call(
        field_kernel,
        [f32(half, block)] * 3,
        [HBM] * 2,
        in_hbm(state), jnp.concatenate([sector_rows, sector_cols]),
        scratch_shapes=[
            pltpu.VMEM((1, block, block), jnp.float32),
            pltpu.SMEM((2,), jnp.int32),
            pltpu.SemaphoreType.DMA((2,)),
        ],
    )
    far, near = neighbours(field)
    left, right = load(left_ops, right_ops, field)
    near, left, right = lax.optimization_barrier((near, left, right))
    halves = [field, field_other, near, swapped(near), far, swapped(far)]
    total, peer = over_chips(*product(term_shift, halves, left, right))

    first = (total + peer) * mask
    far, near = neighbours(first)
    first_other = swapped(first)
    tile = call(tile_kernel, f32(EXTRA, block), [VMEM] * 4, first, first_other, field, field_other)
    tiles = []
    for base in range(1, sectors, ops):
        swaps = [
            (s * ops + a, (s ^ (base + a)) * ops + a if base + a < sectors else (s ^ 1) * ops + a)
            for s in range(sectors)
            for a in range(ops)
        ]
        tiles.append(lax.ppermute(tile, ("sec", "op"), swaps))
    tile = call(
        lambda *refs: gathered_kernel(ops, sectors, *refs),
        f32(EXTRA, block),
        [VMEM] * (1 + len(tiles)),
        tile, *tiles,
    )
    near, tile = lax.optimization_barrier((near, tile))
    halves = [first, first_other, near, swapped(near), far, swapped(far)]
    total, peer = over_chips(*product(term_shift, halves, left, right, tile))

    cells = sectors * block * block
    image = call(
        lambda *refs: image_kernel(cells, *refs),
        f32(half, block),
        [VMEM] * 4,
        total, peer, mask, first,
    )
    correction = call(
        lambda *refs: correction_kernel(cells, *refs),
        f32(1, block, block),
        [VMEM] * 6,
        total, peer, first, first_other, field, field_other,
    )
    image = call(output_kernel, f32(1, block, block), [VMEM] * 2, image, swapped(image))
    return correction, image


def solution(mesh):
    in_specs = (
        P("sec", None, None),
        P("op", "sec", None, None),
        P("op", "sec", None, None),
        P("op"),
        P("sec"),
        P("sec"),
    )
    out_specs = (P("sec", None, None), P("sec", None, None))
    return jax.shard_map(local, mesh=mesh, in_specs=in_specs, out_specs=out_specs, check_vma=False)
```

```python
import jax
import jax.numpy as jnp
from jax import lax
from jax.experimental import pallas as pl
from jax.experimental.pallas import tpu as pltpu
from jax.sharding import PartitionSpec as P

EXTRA = 8
VMEM = pl.BlockSpec(memory_space=pltpu.VMEM)
HBM = pl.BlockSpec(memory_space=pltpu.HBM)


def f32(*shape):
    return jax.ShapeDtypeStruct(shape, jnp.float32)


def in_hbm(x):
    return pltpu.with_memory_space_constraint(x, pltpu.HBM)


def call(kernel, out_shape, in_specs, *arrays, mib=4, **options):
    return pl.pallas_call(
        kernel,
        out_shape=out_shape,
        in_specs=in_specs,
        out_specs=jax.tree.map(lambda _: VMEM, out_shape),
        compiler_params=pltpu.CompilerParams(vmem_limit_bytes=mib * 1024 * 1024),
        **options,
    )(*arrays)


def core_index():
    return lax.rem(lax.axis_index("op"), 2)


def rows_of(core, half):
    return pl.ds(pl.multiple_of(core * half, half), half)


def split(x):
    high = x.astype(jnp.bfloat16)
    low = (x - high.astype(jnp.float32)).astype(jnp.bfloat16)
    return high, low


def dot(a, b, contract):
    return lax.dot_general(
        a, b, (((1,), (contract,)), ((), ())), preferred_element_type=jnp.float32
    )


def total_of(x):
    return jnp.sum(jnp.sum(x, axis=0, keepdims=True), axis=1, keepdims=True)


def field_kernel(state_ref, live_ref, mine_ref, other_ref, mask_ref, state, live, sems):
    copies = [
        pltpu.make_async_copy(ref, buffer, sems.at[i])
        for i, (ref, buffer) in enumerate(
            ((state_ref, state), (live_ref, live))
        )
    ]
    for copy in copies:
        copy.start()
    for copy in copies:
        copy.wait()
    half = mask_ref.shape[0]
    core = core_index()
    rows, cols = live[0], live[1]
    row = lax.broadcasted_iota(jnp.int32, mask_ref.shape, 0)
    lane = lax.broadcasted_iota(jnp.int32, mask_ref.shape, 1)
    for which, ref in ((core, mine_ref), (1 - core, other_ref)):
        inside = (row + which * half < rows) & (lane < cols)
        ref[...] = jnp.where(inside, state[0, rows_of(which, half)], 0.0)
    mask_ref[...] = jnp.where((row + core * half < rows) & (lane < cols), 1.0, 0.0)


def load_kernel(left_ref, right_ref, shift_ref, field_ref, left_out, right_out, shift_out, shift, sems):
    terms = left_ref.shape[0]
    shifts = pltpu.make_async_copy(shift_ref, shift, sems.at[2, 0])
    copies = [
        pltpu.make_async_copy(ref.at[term], out.at[term], sems.at[side, term])
        for term in range(terms)
        for side, (ref, out) in enumerate(((left_ref, left_out), (right_ref, right_out)))
    ]
    shifts.start()
    for copy in copies:
        copy.start()
    shifts.wait()
    for term in range(terms):
        shift_out[term] = jnp.full(shift_out.shape[1:], shift[term], jnp.int32)
    for copy in copies:
        copy.wait()


def load(left_ops, right_ops, shift, field):
    terms = shift.shape[0]
    return call(
        load_kernel,
        [f32(*left_ops.shape), f32(*right_ops.shape), jax.ShapeDtypeStruct((terms, 8, 128), jnp.int32)],
        [HBM, HBM, HBM, VMEM],
        in_hbm(left_ops), in_hbm(right_ops), in_hbm(shift), field,
        scratch_shapes=[pltpu.SMEM(shift.shape, jnp.int32), pltpu.SemaphoreType.DMA((3, terms))],
        cost_estimate=pl.CostEstimate(flops=0, bytes_accessed=8 * left_ops.size, transcendentals=0),
    )


def product_kernel(shift_ref, *refs):
    halves, (left_ref, right_ref) = refs[:6], refs[6:8]
    tile_ref = refs[8] if len(refs) == 14 else None
    send_ref, keep_ref, high, low, total = refs[-5:]
    block = total.shape[0]
    half = block // 2
    core, sector = core_index(), lax.axis_index("sec")
    slot = jnp.where(lax.rem(sector, 2) == 0, 2, 0)
    for index, mine_ref, other_ref in zip((1, slot, 2 - slot), halves[::2], halves[1::2]):
        for which, ref in ((core, mine_ref), (1 - core, other_ref)):
            rows = rows_of(which, half)
            high[index, rows], low[index, rows] = split(ref[...])

    @pl.when(sector == 0)
    def _():
        high[0] = jnp.zeros(high.shape[1:], high.dtype)
        low[0] = jnp.zeros(low.shape[1:], low.dtype)

    @pl.when(sector == lax.axis_size("sec") - 1)
    def _():
        high[2] = jnp.zeros(high.shape[1:], high.dtype)
        low[2] = jnp.zeros(low.shape[1:], low.dtype)

    out = None
    for term in range(left_ref.shape[0]):
        source = 1 - shift_ref[term][0, 0]
        left_high, left_low = split(left_ref[term, 0])
        right_high, right_low = split(right_ref[term, 0])
        v_high, v_low = high[source], low[source]
        inner = dot(left_high, v_high, 0) + (dot(left_low, v_high, 0) + dot(left_high, v_low, 0))
        inner_high, inner_low = split(inner)
        part = dot(inner_high, right_high, 1) + (
            dot(inner_low, right_high, 1) + dot(inner_high, right_low, 1)
        )
        out = part if out is None else out + part
    total[...] = out
    send_ref[pl.ds(0, half)] = total[rows_of(1 - core, half)]
    keep_ref[pl.ds(0, half)] = total[rows_of(core, half)]
    if tile_ref is not None:
        send_ref[pl.ds(half, EXTRA)] = tile_ref[...]
        keep_ref[pl.ds(half, EXTRA)] = tile_ref[...]


def product(shift, halves, left, right, tile=None):
    terms, _, block, _ = left.shape
    rows = block // 2 + (0 if tile is None else EXTRA)
    arrays = [*halves, left, right] + ([] if tile is None else [tile])
    return call(
        product_kernel,
        [f32(rows, block)] * 2,
        [VMEM] * (1 + len(arrays)),
        shift, *arrays,
        mib=16,
        scratch_shapes=[
            pltpu.VMEM((3, block, block), jnp.bfloat16),
            pltpu.VMEM((3, block, block), jnp.bfloat16),
            pltpu.VMEM((block, block), jnp.float32),
        ],
        cost_estimate=pl.CostEstimate(
            flops=12 * terms * block**3, bytes_accessed=4 * left.size, transcendentals=0
        ),
    )


def tile_kernel(first_ref, first_other_ref, field_ref, field_other_ref, out_ref):
    first = jnp.concatenate([first_ref[...], first_other_ref[...]])
    field = jnp.concatenate([field_ref[...], field_other_ref[...]])
    cross, square = total_of(field * first), total_of(field * field)
    theta = jnp.where(square > 0, cross / jnp.where(square > 0, square, 1.0), 0.0)
    resid = first - theta * field
    energy = total_of(resid * resid)
    row = lax.broadcasted_iota(jnp.int32, out_ref.shape, 0)
    lane = lax.broadcasted_iota(jnp.int32, out_ref.shape, 1)
    values = jnp.where(row == 0, cross, jnp.where(row == 1, square, jnp.where(row == 2, energy, 0.0)))
    out_ref[...] = jnp.where(lane == lax.axis_index("sec"), values, 0.0)


def gathered_kernel(planes, tile_ref, *refs):
    *tile_refs, out_ref = refs
    core = core_index()
    total = jnp.where(core == 0, tile_ref[...], 0.0)
    for i, ref in enumerate(tile_refs):
        total = total + jnp.where(1 + 2 * i + core < planes, ref[...], 0.0)
    out_ref[...] = total


def summed_kernel(keep_ref, got_ref, total_ref, sums_ref):
    half = total_ref.shape[0]
    total_ref[...] = keep_ref[pl.ds(0, half)] + got_ref[pl.ds(0, half)]
    sums_ref[...] = keep_ref[pl.ds(half, EXTRA)] + got_ref[pl.ds(half, EXTRA)]


def merged(sums, cells):
    crosses, squares, energies = (sums[i : i + 1] for i in range(3))
    theta = jnp.sum(crosses, axis=1, keepdims=True) / jnp.sum(squares, axis=1, keepdims=True)
    thetas = jnp.where(squares > 0, crosses / jnp.where(squares > 0, squares, 1.0), 0.0)
    energy = jnp.sum(energies + (thetas - theta) ** 2 * squares, axis=1, keepdims=True)
    return theta, lax.rsqrt(energy / cells + 1e-06)


def image_kernel(cells, sums_ref, total_ref, peer_ref, mask_ref, first_ref, out_ref):
    theta, scale = merged(sums_ref[...], cells)
    total = (total_ref[...] + peer_ref[...]) * mask_ref[...]
    out_ref[...] = scale * (total - theta * first_ref[...])


def correction_kernel(cells, sums_ref, first_ref, first_other_ref, field_ref, field_other_ref, out_ref):
    half = first_ref.shape[0]
    core = core_index()
    theta, scale = merged(sums_ref[...], cells)
    out_ref[0, rows_of(core, half)] = scale * (first_ref[...] - theta * field_ref[...])
    out_ref[0, rows_of(1 - core, half)] = scale * (first_other_ref[...] - theta * field_other_ref[...])


def output_kernel(mine_ref, other_ref, out_ref):
    half = mine_ref.shape[0]
    core = core_index()
    out_ref[0, rows_of(core, half)] = mine_ref[...]
    out_ref[0, rows_of(1 - core, half)] = other_ref[...]


def local(state, left_ops, right_ops, term_shift, sector_rows, sector_cols):
    sectors, ops = lax.axis_size("sec"), lax.axis_size("op")
    block = state.shape[1]
    half = block // 2

    others = [(i, i ^ 1) for i in range(ops)]
    pairs = [(s, s ^ 1) for s in range(sectors)]
    between = []
    for a in range(ops):
        between += [(s * ops + a, s * ops + (a ^ 2)) for s in (0, sectors - 1)]
        for s in range(1, sectors - 1, 2):
            between += [(s * ops + a, (s + 1) * ops + a), ((s + 1) * ops + a, s * ops + a)]

    def swapped(v):
        return lax.ppermute(v, "op", others)

    def neighbours(mine):
        return lax.ppermute(mine, ("sec", "op"), between), lax.ppermute(mine, "sec", pairs)

    def over_chips(total):
        step = 2
        while step < ops // 2:
            total = total + lax.ppermute(total, "op", [(i, i ^ step) for i in range(ops)])
            step *= 2
        return total, lax.ppermute(total, "op", [(i, i ^ step) for i in range(ops)])

    field, field_other, mask = call(
        field_kernel,
        [f32(half, block)] * 3,
        [HBM] * 2,
        in_hbm(state), jnp.concatenate([sector_rows, sector_cols]),
        scratch_shapes=[
            pltpu.VMEM((1, block, block), jnp.float32),
            pltpu.SMEM((2,), jnp.int32),
            pltpu.SemaphoreType.DMA((2,)),
        ],
    )
    far, near = neighbours(field)
    left, right, shift = load(left_ops, right_ops, term_shift, field)
    near, left, right = lax.optimization_barrier((near, left, right))
    halves = [field, field_other, near, swapped(near), far, swapped(far)]
    send, keep = product(shift, halves, left, right)
    total, peer = over_chips(keep + swapped(send))

    first = (total + peer) * mask
    far, near = neighbours(first)
    first_other = swapped(first)
    tile = call(tile_kernel, f32(EXTRA, block), [VMEM] * 4, first, first_other, field, field_other)
    planes = sectors // 2
    tiles = []
    for base in range(1, planes, 2):
        swaps = [
            (s * ops + a, (s ^ (2 * (base + a % 2) if base + a % 2 < planes else 2)) * ops + a)
            for s in range(sectors)
            for a in range(ops)
        ]
        tiles.append(lax.ppermute(tile, ("sec", "op"), swaps))
    tile = call(
        lambda *refs: gathered_kernel(planes, *refs),
        f32(EXTRA, block),
        [VMEM] * (1 + len(tiles)),
        tile, *tiles,
    )
    near, tile = lax.optimization_barrier((near, tile))
    halves = [first, first_other, near, swapped(near), far, swapped(far)]
    send, keep = product(shift, halves, left, right, tile)
    total, sums = call(
        summed_kernel, [f32(half, block), f32(EXTRA, block)], [VMEM] * 2, keep, swapped(send)
    )
    total, peer = over_chips(total)
    sums = sums + lax.ppermute(sums, "sec", pairs)

    cells = sectors * block * block
    image = call(
        lambda *refs: image_kernel(cells, *refs),
        f32(half, block),
        [VMEM] * 5,
        sums, total, peer, mask, first,
    )
    correction = call(
        lambda *refs: correction_kernel(cells, *refs),
        f32(1, block, block),
        [VMEM] * 5,
        sums, first, first_other, field, field_other,
    )
    image = call(output_kernel, f32(1, block, block), [VMEM] * 2, image, swapped(image))
    return correction, image


def solution(mesh):
    in_specs = (
        P("sec", None, None),
        P("op", "sec", None, None),
        P("op", "sec", None, None),
        P("op"),
        P("sec"),
        P("sec"),
    )
    out_specs = (P("sec", None, None), P("sec", None, None))
    return jax.shard_map(local, mesh=mesh, in_specs=in_specs, out_specs=out_specs, check_vma=False)
```

```python
import jax
import jax.numpy as jnp
from jax import lax
from jax.experimental import pallas as pl
from jax.experimental.pallas import tpu as pltpu
from jax.sharding import PartitionSpec as P

EXTRA = 8
VMEM = pl.BlockSpec(memory_space=pltpu.VMEM)
HBM = pl.BlockSpec(memory_space=pltpu.HBM)


def f32(*shape):
    return jax.ShapeDtypeStruct(shape, jnp.float32)


def in_hbm(x):
    return pltpu.with_memory_space_constraint(x, pltpu.HBM)


def call(kernel, out_shape, in_specs, *arrays, mib=4, **options):
    return pl.pallas_call(
        kernel,
        out_shape=out_shape,
        in_specs=in_specs,
        out_specs=jax.tree.map(lambda _: VMEM, out_shape),
        compiler_params=pltpu.CompilerParams(vmem_limit_bytes=mib * 1024 * 1024),
        **options,
    )(*arrays)


def core_index():
    return lax.rem(lax.axis_index("op"), 2)


def rows_of(core, half):
    return pl.ds(pl.multiple_of(core * half, half), half)


def split(x):
    high = x.astype(jnp.bfloat16)
    low = (x - high.astype(jnp.float32)).astype(jnp.bfloat16)
    return high, low


def dot(a, b, contract):
    return lax.dot_general(
        a, b, (((1,), (contract,)), ((), ())), preferred_element_type=jnp.float32
    )


def total_of(x):
    return jnp.sum(jnp.sum(x, axis=0, keepdims=True), axis=1, keepdims=True)


def inside(shape, first_row, rows, cols):
    row = lax.broadcasted_iota(jnp.int32, shape, 0) + first_row
    return (row < rows) & (lax.broadcasted_iota(jnp.int32, shape, 1) < cols)


def field_kernel(state_ref, live_ref, field_ref, other_ref, mask_ref, live_out, state, live, sems):
    copies = [
        pltpu.make_async_copy(ref, buffer, sems.at[i])
        for i, (ref, buffer) in enumerate(((state_ref, state), (live_ref, live)))
    ]
    for copy in copies:
        copy.start()
    for copy in copies:
        copy.wait()
    half = mask_ref.shape[0]
    core = core_index()
    rows, cols = live[0], live[1]
    for which, ref in ((core, field_ref), (1 - core, other_ref)):
        start = which * half
        ref[...] = jnp.where(inside(ref.shape, start, rows, cols), state[0, rows_of(which, half)], 0.0)
    mask_ref[...] = jnp.where(inside(mask_ref.shape, core * half, rows, cols), 1.0, 0.0)
    row = lax.broadcasted_iota(jnp.int32, live_out.shape, 0)
    live_out[...] = jnp.where(row == 0, rows, cols)


def load_kernel(left_ref, right_ref, shift_ref, field_ref, left_out, right_out, shift_out, shift, sems):
    terms = left_ref.shape[0]
    shifts = pltpu.make_async_copy(shift_ref, shift, sems.at[2, 0])
    copies = [
        pltpu.make_async_copy(ref.at[term], out.at[term], sems.at[side, term])
        for term in range(terms)
        for side, (ref, out) in enumerate(((left_ref, left_out), (right_ref, right_out)))
    ]
    shifts.start()
    for copy in copies:
        copy.start()
    shifts.wait()
    for term in range(terms):
        shift_out[term] = jnp.full(shift_out.shape[1:], shift[term], jnp.int32)
    for copy in copies:
        copy.wait()


def load(left_ops, right_ops, shift, field):
    terms = shift.shape[0]
    return call(
        load_kernel,
        [f32(*left_ops.shape), f32(*right_ops.shape), jax.ShapeDtypeStruct((terms, 8, 128), jnp.int32)],
        [HBM, HBM, HBM, VMEM],
        in_hbm(left_ops), in_hbm(right_ops), in_hbm(shift), field,
        scratch_shapes=[pltpu.SMEM(shift.shape, jnp.int32), pltpu.SemaphoreType.DMA((3, terms))],
        cost_estimate=pl.CostEstimate(flops=0, bytes_accessed=8 * left_ops.size, transcendentals=0),
    )


def product_kernel(raw, tiled, shift_ref, *refs):
    left_ref, right_ref, own_refs, refs = *refs[:2], refs[2:4], refs[4:]
    send_ref, keep_ref, high, low, total = refs[-5:]
    block = total.shape[0]
    half = block // 2
    core, sector = core_index(), lax.axis_index("sec")
    slot = jnp.where(lax.rem(sector, 2) == 0, 2, 0)

    def put(index, pair_of_refs):
        for which, ref in zip((core, 1 - core), pair_of_refs):
            rows = rows_of(which, half)
            high[index, rows], low[index, rows] = split(ref[...])

    put(1, own_refs)
    if raw:
        got = jnp.where(core == 0, slot, 2 - slot)
        for index, ref, live_ref in zip((got, 2 - got), refs[:2], refs[2:4]):
            live = inside((block, block), 0, live_ref[:1, :1], live_ref[1:2, :1])
            high[index], low[index] = split(jnp.where(live, ref[...], 0.0))
    else:
        put(slot, refs[:2])
        put(2 - slot, refs[2:4])

    @pl.when(sector == 0)
    def _():
        high[0] = jnp.zeros(high.shape[1:], high.dtype)
        low[0] = jnp.zeros(low.shape[1:], low.dtype)

    @pl.when(sector == lax.axis_size("sec") - 1)
    def _():
        high[2] = jnp.zeros(high.shape[1:], high.dtype)
        low[2] = jnp.zeros(low.shape[1:], low.dtype)

    out = None
    for term in range(left_ref.shape[0]):
        source = 1 - shift_ref[term][0, 0]
        left_high, left_low = split(left_ref[term, 0])
        right_high, right_low = split(right_ref[term, 0])
        v_high, v_low = high[source], low[source]
        inner = dot(left_high, v_high, 0) + (dot(left_low, v_high, 0) + dot(left_high, v_low, 0))
        inner_high, inner_low = split(inner)
        part = dot(inner_high, right_high, 1) + (
            dot(inner_low, right_high, 1) + dot(inner_high, right_low, 1)
        )
        out = part if out is None else out + part
    total[...] = out
    send_ref[pl.ds(0, half)] = total[rows_of(1 - core, half)]
    keep_ref[pl.ds(0, half)] = total[rows_of(core, half)]
    if tiled:
        send_ref[pl.ds(half, EXTRA)] = refs[4][...]
        keep_ref[pl.ds(half, EXTRA)] = refs[4][...]


def product(shift, left, right, *arrays, raw=False, tiled=False):
    terms, _, block, _ = left.shape
    arrays = [shift, left, right, *arrays]
    return call(
        lambda *refs: product_kernel(raw, tiled, *refs),
        [f32(block // 2 + (EXTRA if tiled else 0), block)] * 2,
        [VMEM] * len(arrays),
        *arrays,
        mib=16,
        scratch_shapes=[
            pltpu.VMEM((3, block, block), jnp.bfloat16),
            pltpu.VMEM((3, block, block), jnp.bfloat16),
            pltpu.VMEM((block, block), jnp.float32),
        ],
        cost_estimate=pl.CostEstimate(
            flops=12 * terms * block**3, bytes_accessed=4 * left.size, transcendentals=0
        ),
    )


def tile_kernel(first_ref, first_other_ref, field_ref, field_other_ref, out_ref):
    first = jnp.concatenate([first_ref[...], first_other_ref[...]])
    field = jnp.concatenate([field_ref[...], field_other_ref[...]])
    cross, square = total_of(field * first), total_of(field * field)
    theta = jnp.where(square > 0, cross / jnp.where(square > 0, square, 1.0), 0.0)
    resid = first - theta * field
    energy = total_of(resid * resid)
    row = lax.broadcasted_iota(jnp.int32, out_ref.shape, 0)
    lane = lax.broadcasted_iota(jnp.int32, out_ref.shape, 1)
    values = jnp.where(row == 0, cross, jnp.where(row == 1, square, jnp.where(row == 2, energy, 0.0)))
    out_ref[...] = jnp.where(lane == lax.axis_index("sec"), values, 0.0)


def gathered_kernel(planes, tile_ref, *refs):
    *tile_refs, out_ref = refs
    core = core_index()
    total = jnp.where(core == 0, tile_ref[...], 0.0)
    for i, ref in enumerate(tile_refs):
        total = total + jnp.where(1 + 2 * i + core < planes, ref[...], 0.0)
    out_ref[...] = total


def summed_kernel(keep_ref, got_ref, total_ref, sums_ref):
    half = total_ref.shape[0]
    total_ref[...] = keep_ref[pl.ds(0, half)] + got_ref[pl.ds(0, half)]
    sums_ref[...] = keep_ref[pl.ds(half, EXTRA)] + got_ref[pl.ds(half, EXTRA)]


def merged_kernel(cells, sums_ref, got_ref, out_ref):
    sums = sums_ref[...] + got_ref[...]
    crosses, squares, energies = (sums[i : i + 1] for i in range(3))
    theta = jnp.sum(crosses, axis=1, keepdims=True) / jnp.sum(squares, axis=1, keepdims=True)
    thetas = jnp.where(squares > 0, crosses / jnp.where(squares > 0, squares, 1.0), 0.0)
    energy = jnp.sum(energies + (thetas - theta) ** 2 * squares, axis=1, keepdims=True)
    scale = lax.rsqrt(energy / cells + 1e-06)
    row = lax.broadcasted_iota(jnp.int32, out_ref.shape, 0)
    out_ref[...] = jnp.where(row == 0, theta, scale)


def image_kernel(merged_ref, total_ref, peer_ref, mask_ref, first_ref, out_ref):
    theta, scale = merged_ref[0:1, :], merged_ref[1:2, :]
    total = (total_ref[...] + peer_ref[...]) * mask_ref[...]
    out_ref[...] = scale * (total - theta * first_ref[...])


def correction_kernel(merged_ref, first_ref, first_other_ref, field_ref, field_other_ref, out_ref):
    half = first_ref.shape[0]
    core = core_index()
    theta, scale = merged_ref[0:1, :], merged_ref[1:2, :]
    out_ref[0, rows_of(core, half)] = scale * (first_ref[...] - theta * field_ref[...])
    out_ref[0, rows_of(1 - core, half)] = scale * (first_other_ref[...] - theta * field_other_ref[...])


def output_kernel(mine_ref, other_ref, out_ref):
    half = mine_ref.shape[0]
    core = core_index()
    out_ref[0, rows_of(core, half)] = mine_ref[...]
    out_ref[0, rows_of(1 - core, half)] = other_ref[...]


def local(state, left_ops, right_ops, term_shift, sector_rows, sector_cols):
    sectors, ops = lax.axis_size("sec"), lax.axis_size("op")
    block = state.shape[1]
    half = block // 2

    others = [(i, i ^ 1) for i in range(ops)]
    pairs = [(s, s ^ 1) for s in range(sectors)]
    between = []
    for a in range(ops):
        between += [(s * ops + a, s * ops + (a ^ 2)) for s in (0, sectors - 1)]
        for s in range(1, sectors - 1, 2):
            between += [(s * ops + a, (s + 1) * ops + a), ((s + 1) * ops + a, s * ops + a)]

    def swapped(v):
        return lax.ppermute(v, "op", others)

    def neighbours(mine):
        return lax.ppermute(mine, ("sec", "op"), between), lax.ppermute(mine, "sec", pairs)

    def over_chips(total):
        step = 2
        while step < ops // 2:
            total = total + lax.ppermute(total, "op", [(i, i ^ step) for i in range(ops)])
            step *= 2
        return total, lax.ppermute(total, "op", [(i, i ^ step) for i in range(ops)])

    crossing = [(s * ops + a, (s ^ 1) * ops + a) for s in range(sectors) for a in range(0, ops, 2)]
    crossing += [(source, target) for source, target in between if source % 2]
    got = lax.ppermute(state[0], ("sec", "op"), crossing)
    field, field_other, mask, live = call(
        field_kernel,
        [f32(half, block)] * 3 + [jax.ShapeDtypeStruct((8, 128), jnp.int32)],
        [HBM] * 2,
        in_hbm(state), jnp.concatenate([sector_rows, sector_cols]),
        scratch_shapes=[
            pltpu.VMEM((1, block, block), jnp.float32),
            pltpu.SMEM((2,), jnp.int32),
            pltpu.SemaphoreType.DMA((2,)),
        ],
    )
    live = lax.ppermute(live, ("sec", "op"), crossing)
    left, right, shift = load(left_ops, right_ops, term_shift, field)
    got, left, right, live = lax.optimization_barrier((got, left, right, live))
    send, keep = product(
        shift, left, right, field, field_other, got, swapped(got), live, swapped(live), raw=True
    )
    total, peer = over_chips(keep + swapped(send))

    first = (total + peer) * mask
    far, near = neighbours(first)
    first_other = swapped(first)
    tile = call(tile_kernel, f32(EXTRA, block), [VMEM] * 4, first, first_other, field, field_other)
    planes = sectors // 2
    tiles = []
    for base in range(1, planes, 2):
        swaps = [
            (s * ops + a, (s ^ (2 * (base + a % 2) if base + a % 2 < planes else 2)) * ops + a)
            for s in range(sectors)
            for a in range(ops)
        ]
        tiles.append(lax.ppermute(tile, ("sec", "op"), swaps))
    tile = call(
        lambda *refs: gathered_kernel(planes, *refs),
        f32(EXTRA, block),
        [VMEM] * (1 + len(tiles)),
        tile, *tiles,
    )
    near, tile = lax.optimization_barrier((near, tile))
    send, keep = product(
        shift, left, right, first, first_other, near, swapped(near), far, swapped(far), tile, tiled=True
    )
    total, sums = call(
        summed_kernel, [f32(half, block), f32(EXTRA, block)], [VMEM] * 2, keep, swapped(send)
    )
    total, peer = over_chips(total)

    cells = sectors * block * block
    merged = call(
        lambda *refs: merged_kernel(cells, *refs),
        f32(EXTRA, block),
        [VMEM] * 2,
        sums, lax.ppermute(sums, "sec", pairs),
    )
    image = call(image_kernel, f32(half, block), [VMEM] * 5, merged, total, peer, mask, first)
    correction = call(
        correction_kernel,
        f32(1, block, block),
        [VMEM] * 5,
        merged, first, first_other, field, field_other,
    )
    image = call(output_kernel, f32(1, block, block), [VMEM] * 2, image, swapped(image))
    return correction, image


def solution(mesh):
    in_specs = (
        P("sec", None, None),
        P("op", "sec", None, None),
        P("op", "sec", None, None),
        P("op"),
        P("sec"),
        P("sec"),
    )
    out_specs = (P("sec", None, None), P("sec", None, None))
    return jax.shard_map(local, mesh=mesh, in_specs=in_specs, out_specs=out_specs, check_vma=False)
```

```python
import jax
import jax.numpy as jnp
from jax import lax
from jax.experimental import pallas as pl
from jax.experimental.pallas import tpu as pltpu
from jax.sharding import PartitionSpec as P

EXTRA = 8
VMEM = pl.BlockSpec(memory_space=pltpu.VMEM)
HBM = pl.BlockSpec(memory_space=pltpu.HBM)


def f32(*shape):
    return jax.ShapeDtypeStruct(shape, jnp.float32)


def in_hbm(x):
    return pltpu.with_memory_space_constraint(x, pltpu.HBM)


def call(kernel, out_shape, in_specs, *arrays, mib=4, **options):
    return pl.pallas_call(
        kernel,
        out_shape=out_shape,
        in_specs=in_specs,
        out_specs=jax.tree.map(lambda _: VMEM, out_shape),
        compiler_params=pltpu.CompilerParams(vmem_limit_bytes=mib * 1024 * 1024),
        **options,
    )(*arrays)


def core_index():
    return lax.rem(lax.axis_index("op"), 2)


def rows_of(core, half):
    return pl.ds(pl.multiple_of(core * half, half), half)


def split(x):
    high = x.astype(jnp.bfloat16)
    low = (x - high.astype(jnp.float32)).astype(jnp.bfloat16)
    return high, low


def dot(a, b, contract):
    return lax.dot_general(
        a, b, (((1,), (contract,)), ((), ())), preferred_element_type=jnp.float32
    )


def total_of(x):
    return jnp.sum(jnp.sum(x, axis=0, keepdims=True), axis=1, keepdims=True)


def inside(shape, first_row, rows, cols):
    row = lax.broadcasted_iota(jnp.int32, shape, 0) + first_row
    return (row < rows) & (lax.broadcasted_iota(jnp.int32, shape, 1) < cols)


def field_kernel(state_ref, live_ref, field_ref, other_ref, mask_ref, live_out, state, live, sems):
    copies = [
        pltpu.make_async_copy(ref, buffer, sems.at[i])
        for i, (ref, buffer) in enumerate(((state_ref, state), (live_ref, live)))
    ]
    for copy in copies:
        copy.start()
    for copy in copies:
        copy.wait()
    half = mask_ref.shape[0]
    core = core_index()
    rows, cols = live[0], live[1]
    for which, ref in ((core, field_ref), (1 - core, other_ref)):
        start = which * half
        ref[...] = jnp.where(inside(ref.shape, start, rows, cols), state[0, rows_of(which, half)], 0.0)
    mask_ref[...] = jnp.where(inside(mask_ref.shape, core * half, rows, cols), 1.0, 0.0)
    row = lax.broadcasted_iota(jnp.int32, live_out.shape, 0)
    live_out[...] = jnp.where(row == 0, rows, cols)


def load_kernel(left_ref, right_ref, shift_ref, field_ref, left_out, right_out, shift_out, shift, sems):
    terms = left_ref.shape[0]
    shifts = pltpu.make_async_copy(shift_ref, shift, sems.at[2, 0])
    copies = [
        pltpu.make_async_copy(ref.at[term], out.at[term], sems.at[side, term])
        for term in range(terms)
        for side, (ref, out) in enumerate(((left_ref, left_out), (right_ref, right_out)))
    ]
    shifts.start()
    for copy in copies:
        copy.start()
    shifts.wait()
    for term in range(terms):
        shift_out[term] = jnp.full(shift_out.shape[1:], shift[term], jnp.int32)
    for copy in copies:
        copy.wait()


def load(left_ops, right_ops, shift, field):
    terms = shift.shape[0]
    return call(
        load_kernel,
        [f32(*left_ops.shape), f32(*right_ops.shape), jax.ShapeDtypeStruct((terms, 8, 128), jnp.int32)],
        [HBM, HBM, HBM, VMEM],
        in_hbm(left_ops), in_hbm(right_ops), in_hbm(shift), field,
        scratch_shapes=[pltpu.SMEM(shift.shape, jnp.int32), pltpu.SemaphoreType.DMA((3, terms))],
        cost_estimate=pl.CostEstimate(flops=0, bytes_accessed=8 * left_ops.size, transcendentals=0),
    )


def half_product(which, shift_ref, high, low, left_ref, right_ref):
    half = left_ref.shape[2] // 2
    rows = rows_of(which, half)

    def thrice(a, b, contract):
        (a_high, a_low), (b_high, b_low) = a, b
        both = dot(jnp.concatenate([a_high, a_low]), b_high, contract)
        return both[:half] + (both[half:] + dot(a_high, b_low, contract))

    inner = []
    for term in range(left_ref.shape[0]):
        source = 1 - shift_ref[term][0, 0]
        inner.append(thrice(split(left_ref[term, 0, rows]), (high[source], low[source]), 0))
    out = None
    for term in range(right_ref.shape[0]):
        part = thrice(split(inner[term]), split(right_ref[term, 0]), 1)
        out = part if out is None else out + part
    return out


def send_kernel(raw, shift_ref, left_ref, right_ref, own_ref, own_other_ref, *refs):
    *refs, send_ref, high, low = refs
    half, block = send_ref.shape
    core, sector = core_index(), lax.axis_index("sec")
    slot = jnp.where(lax.rem(sector, 2) == 0, 2, 0)
    got = jnp.where(core == 1, slot, 2 - slot)

    def put(index, mine_ref, other_ref):
        for which, ref in ((core, mine_ref), (1 - core, other_ref)):
            rows = rows_of(which, half)
            high[index, rows], low[index, rows] = split(ref[...])

    put(1, own_ref, own_other_ref)
    if raw:
        for index, ref, live_ref in zip((got, 2 - got), refs[:2], refs[2:]):
            live = inside((block, block), 0, live_ref[:1, :1], live_ref[1:2, :1])
            high[index], low[index] = split(jnp.where(live, ref[...], 0.0))
    else:
        one_ref, one_other_ref, two_ref, two_other_ref = refs
        put(got, one_ref, two_other_ref)
        put(2 - got, two_ref, one_other_ref)

    @pl.when(sector == 0)
    def _():
        high[0] = jnp.zeros(high.shape[1:], high.dtype)
        low[0] = jnp.zeros(low.shape[1:], low.dtype)

    @pl.when(sector == lax.axis_size("sec") - 1)
    def _():
        high[2] = jnp.zeros(high.shape[1:], high.dtype)
        low[2] = jnp.zeros(low.shape[1:], low.dtype)

    send_ref[...] = half_product(1 - core, shift_ref, high, low, left_ref, right_ref)


def keep_kernel(shift_ref, left_ref, right_ref, high, low, *refs):
    refs[-1][...] = half_product(core_index(), shift_ref, high, low, left_ref, right_ref)


def product_options(left):
    terms, _, block, _ = left.shape
    return dict(
        mib=16,
        cost_estimate=pl.CostEstimate(
            flops=30 * terms * block**3, bytes_accessed=8 * left.size, transcendentals=0
        ),
    )


def product_to_send(shift, left, right, *arrays, raw=False):
    block = left.shape[-1]
    arrays = [shift, left, right, *arrays]
    return call(
        lambda *refs: send_kernel(raw, *refs),
        [f32(block // 2, block)] + [jax.ShapeDtypeStruct((3, block, block), jnp.bfloat16)] * 2,
        [VMEM] * len(arrays),
        *arrays,
        **product_options(left),
    )


def product_to_keep(shift, left, right, high, low, *after):
    block = left.shape[-1]
    arrays = [shift, left, right, high, low, *after]
    return call(
        keep_kernel, f32(block // 2, block), [VMEM] * len(arrays), *arrays, **product_options(left)
    )


def tile_kernel(first_ref, first_other_ref, field_ref, field_other_ref, out_ref):
    first = jnp.concatenate([first_ref[...], first_other_ref[...]])
    field = jnp.concatenate([field_ref[...], field_other_ref[...]])
    cross, square = total_of(field * first), total_of(field * field)
    theta = jnp.where(square > 0, cross / jnp.where(square > 0, square, 1.0), 0.0)
    resid = first - theta * field
    energy = total_of(resid * resid)
    row = lax.broadcasted_iota(jnp.int32, out_ref.shape, 0)
    lane = lax.broadcasted_iota(jnp.int32, out_ref.shape, 1)
    values = jnp.where(row == 0, cross, jnp.where(row == 1, square, jnp.where(row == 2, energy, 0.0)))
    out_ref[...] = jnp.where(lane == lax.axis_index("sec"), values, 0.0)


def added_kernel(a_ref, b_ref, after_ref, out_ref):
    out_ref[...] = a_ref[...] + b_ref[...]


def merged_kernel(cells, sums_ref, got_ref, out_ref):
    sums = sums_ref[...] + got_ref[...]
    crosses, squares, energies = (sums[i : i + 1] for i in range(3))
    theta = jnp.sum(crosses, axis=1, keepdims=True) / jnp.sum(squares, axis=1, keepdims=True)
    thetas = jnp.where(squares > 0, crosses / jnp.where(squares > 0, squares, 1.0), 0.0)
    energy = jnp.sum(energies + (thetas - theta) ** 2 * squares, axis=1, keepdims=True)
    scale = lax.rsqrt(energy / cells + 1e-06)
    row = lax.broadcasted_iota(jnp.int32, out_ref.shape, 0)
    out_ref[...] = jnp.where(row == 0, theta, scale)


def image_kernel(merged_ref, total_ref, peer_ref, mask_ref, first_ref, out_ref):
    theta, scale = merged_ref[0:1, :], merged_ref[1:2, :]
    total = (total_ref[...] + peer_ref[...]) * mask_ref[...]
    out_ref[...] = scale * (total - theta * first_ref[...])


def correction_kernel(merged_ref, first_ref, first_other_ref, field_ref, field_other_ref, out_ref):
    half = first_ref.shape[0]
    core = core_index()
    theta, scale = merged_ref[0:1, :], merged_ref[1:2, :]
    out_ref[0, rows_of(core, half)] = scale * (first_ref[...] - theta * field_ref[...])
    out_ref[0, rows_of(1 - core, half)] = scale * (first_other_ref[...] - theta * field_other_ref[...])


def output_kernel(mine_ref, other_ref, out_ref):
    half = mine_ref.shape[0]
    core = core_index()
    out_ref[0, rows_of(core, half)] = mine_ref[...]
    out_ref[0, rows_of(1 - core, half)] = other_ref[...]


def local(state, left_ops, right_ops, term_shift, sector_rows, sector_cols):
    sectors, ops = lax.axis_size("sec"), lax.axis_size("op")
    block = state.shape[1]
    half = block // 2

    others = [(i, i ^ 1) for i in range(ops)]
    pairs = [(s, s ^ 1) for s in range(sectors)]
    between = []
    for a in range(ops):
        between += [(s * ops + a, s * ops + (a ^ 2)) for s in (0, sectors - 1)]
        for s in range(1, sectors - 1, 2):
            between += [(s * ops + a, (s + 1) * ops + a), ((s + 1) * ops + a, s * ops + a)]

    def swapped(v):
        return lax.ppermute(v, "op", others)

    def over_chips(total):
        step = 2
        while step < ops // 2:
            total = total + lax.ppermute(total, "op", [(i, i ^ step) for i in range(ops)])
            step *= 2
        return total, lax.ppermute(total, "op", [(i, i ^ step) for i in range(ops)])

    crossing = [(s * ops + a, (s ^ 1) * ops + a) for s in range(sectors) for a in range(1, ops, 2)]
    crossing += [(source, target) for source, target in between if source % 2 == 0]
    crossing_too = [(s * ops + a, (s ^ 1) * ops + a) for s in range(sectors) for a in range(0, ops, 2)]
    crossing_too += [(source, target) for source, target in between if source % 2]
    got = lax.ppermute(state[0], ("sec", "op"), crossing)
    field, field_other, mask, live = call(
        field_kernel,
        [f32(half, block)] * 3 + [jax.ShapeDtypeStruct((8, 128), jnp.int32)],
        [HBM] * 2,
        in_hbm(state), jnp.concatenate([sector_rows, sector_cols]),
        scratch_shapes=[
            pltpu.VMEM((1, block, block), jnp.float32),
            pltpu.SMEM((2,), jnp.int32),
            pltpu.SemaphoreType.DMA((2,)),
        ],
    )
    live = lax.ppermute(live, ("sec", "op"), crossing)
    left, right, shift = load(left_ops, right_ops, term_shift, field)
    got, left, right, live = lax.optimization_barrier((got, left, right, live))
    send, *parts = product_to_send(
        shift, left, right, field, field_other, got, swapped(got), live, swapped(live), raw=True
    )
    total, peer = over_chips(product_to_keep(shift, left, right, *parts) + swapped(send))

    first = (total + peer) * mask
    one = lax.ppermute(first, ("sec", "op"), crossing)
    two = lax.ppermute(first, ("sec", "op"), crossing_too)
    first_other = swapped(first)
    sums = call(tile_kernel, f32(EXTRA, block), [VMEM] * 4, first, first_other, field, field_other)

    def with_distant(sums, step):
        return sums + lax.ppermute(sums, "sec", [(s, s ^ step) for s in range(sectors)])

    step = sectors // 2
    while step > 2:
        sums = with_distant(sums, step)
        step //= 2
    two, sums = lax.optimization_barrier((two, sums))
    send, *parts = product_to_send(
        shift, left, right, first, first_other, one, swapped(one), two, swapped(two)
    )
    sums = call(
        added_kernel,
        f32(EXTRA, block),
        [VMEM] * 3,
        sums, lax.ppermute(sums, "sec", [(s, s ^ 2) for s in range(sectors)]), send,
    )
    keep = product_to_keep(shift, left, right, *parts, sums)
    total, peer = over_chips(keep + swapped(send))

    cells = sectors * block * block
    merged = call(
        lambda *refs: merged_kernel(cells, *refs),
        f32(EXTRA, block),
        [VMEM] * 2,
        sums, lax.ppermute(sums, "sec", pairs),
    )
    image = call(image_kernel, f32(half, block), [VMEM] * 5, merged, total, peer, mask, first)
    correction = call(
        correction_kernel,
        f32(1, block, block),
        [VMEM] * 5,
        merged, first, first_other, field, field_other,
    )
    image = call(output_kernel, f32(1, block, block), [VMEM] * 2, image, swapped(image))
    return correction, image


def solution(mesh):
    in_specs = (
        P("sec", None, None),
        P("op", "sec", None, None),
        P("op", "sec", None, None),
        P("op"),
        P("sec"),
        P("sec"),
    )
    out_specs = (P("sec", None, None), P("sec", None, None))
    return jax.shard_map(local, mesh=mesh, in_specs=in_specs, out_specs=out_specs, check_vma=False)
```

```python
import jax
import jax.numpy as jnp
from jax import lax
from jax.experimental import pallas as pl
from jax.experimental.pallas import tpu as pltpu
from jax.sharding import PartitionSpec as P

EXTRA = 8
VMEM = pl.BlockSpec(memory_space=pltpu.VMEM)
HBM = pl.BlockSpec(memory_space=pltpu.HBM)


def f32(*shape):
    return jax.ShapeDtypeStruct(shape, jnp.float32)


def in_hbm(x):
    return pltpu.with_memory_space_constraint(x, pltpu.HBM)


def call(kernel, out_shape, in_specs, *arrays, mib=4, **options):
    return pl.pallas_call(
        kernel,
        out_shape=out_shape,
        in_specs=in_specs,
        out_specs=jax.tree.map(lambda _: VMEM, out_shape),
        compiler_params=pltpu.CompilerParams(vmem_limit_bytes=mib * 1024 * 1024),
        **options,
    )(*arrays)


def core_index():
    return lax.rem(lax.axis_index("op"), 2)


def rows_of(core, half):
    return pl.ds(pl.multiple_of(core * half, half), half)


def split(x):
    high = x.astype(jnp.bfloat16)
    low = (x - high.astype(jnp.float32)).astype(jnp.bfloat16)
    return high, low


def dot(a, b):
    return jnp.dot(a, b, preferred_element_type=jnp.float32)


def total_of(x):
    return jnp.sum(jnp.sum(x, axis=0, keepdims=True), axis=1, keepdims=True)


def inside(shape, first_row, rows, cols):
    row = lax.broadcasted_iota(jnp.int32, shape, 0) + first_row
    return (row < rows) & (lax.broadcasted_iota(jnp.int32, shape, 1) < cols)


def field_kernel(state_ref, live_ref, field_ref, other_ref, mask_ref, live_out, state, live, sems):
    copies = [
        pltpu.make_async_copy(ref, buffer, sems.at[i])
        for i, (ref, buffer) in enumerate(((state_ref, state), (live_ref, live)))
    ]
    for copy in copies:
        copy.start()
    for copy in copies:
        copy.wait()
    half = mask_ref.shape[0]
    core = core_index()
    rows, cols = live[0], live[1]
    for which, ref in ((core, field_ref), (1 - core, other_ref)):
        start = which * half
        ref[...] = jnp.where(inside(ref.shape, start, rows, cols), state[0, rows_of(which, half)], 0.0)
    mask_ref[...] = jnp.where(inside(mask_ref.shape, core * half, rows, cols), 1.0, 0.0)
    row = lax.broadcasted_iota(jnp.int32, live_out.shape, 0)
    live_out[...] = jnp.where(row == 0, rows, cols)


def load_kernel(left_ref, right_ref, shift_ref, field_ref, left_out, right_out, shift_out, right, shift, sems):
    terms = left_ref.shape[0]
    shifts = pltpu.make_async_copy(shift_ref, shift, sems.at[2, 0])
    rights = [
        pltpu.make_async_copy(right_ref.at[term], right.at[term], sems.at[0, term])
        for term in range(terms)
    ]
    lefts = [
        pltpu.make_async_copy(left_ref.at[term], left_out.at[term], sems.at[1, term])
        for term in range(terms)
    ]
    for copy in (shifts, *rights, *lefts):
        copy.start()
    shifts.wait()
    for term in range(terms):
        shift_out[term] = jnp.full(shift_out.shape[1:], shift[term], jnp.int32)
    for term in range(terms):
        rights[term].wait()
        right_out[term, 0] = right[term, 0].T
    for copy in lefts:
        copy.wait()


def load(left_ops, right_ops, shift, field):
    terms = shift.shape[0]
    return call(
        load_kernel,
        [f32(*left_ops.shape), f32(*right_ops.shape), jax.ShapeDtypeStruct((terms, 8, 128), jnp.int32)],
        [HBM, HBM, HBM, VMEM],
        in_hbm(left_ops), in_hbm(right_ops), in_hbm(shift), field,
        mib=8,
        scratch_shapes=[
            pltpu.VMEM(right_ops.shape, jnp.float32),
            pltpu.SMEM(shift.shape, jnp.int32),
            pltpu.SemaphoreType.DMA((3, terms)),
        ],
        cost_estimate=pl.CostEstimate(flops=0, bytes_accessed=8 * left_ops.size, transcendentals=0),
    )


def half_product(which, shift_ref, high, low, left_ref, right_ref):
    half = left_ref.shape[2] // 2
    rows = rows_of(which, half)

    def thrice(a, b):
        (a_high, a_low), (b_high, b_low) = a, b
        both = dot(jnp.concatenate([a_high, a_low]), b_high)
        return both[:half] + (both[half:] + dot(a_high, b_low))

    inner = []
    for term in range(left_ref.shape[0]):
        source = 1 - shift_ref[term][0, 0]
        inner.append(thrice(split(left_ref[term, 0, rows]), (high[source], low[source])))
    out = None
    for term in range(right_ref.shape[0]):
        part = thrice(split(inner[term]), split(right_ref[term, 0]))
        out = part if out is None else out + part
    return out


def send_kernel(raw, shift_ref, left_ref, right_ref, own_ref, own_other_ref, *refs):
    *refs, send_ref, high, low = refs
    half, block = send_ref.shape
    core, sector = core_index(), lax.axis_index("sec")
    slot = jnp.where(lax.rem(sector, 2) == 0, 2, 0)
    got = jnp.where(core == 1, slot, 2 - slot)

    def put(index, mine_ref, other_ref):
        for which, ref in ((core, mine_ref), (1 - core, other_ref)):
            rows = rows_of(which, half)
            high[index, rows], low[index, rows] = split(ref[...])

    put(1, own_ref, own_other_ref)
    if raw:
        for index, ref, live_ref in zip((got, 2 - got), refs[:2], refs[2:]):
            live = inside((block, block), 0, live_ref[:1, :1], live_ref[1:2, :1])
            high[index], low[index] = split(jnp.where(live, ref[...], 0.0))
    else:
        one_ref, one_other_ref, two_ref, two_other_ref = refs
        put(got, one_ref, two_other_ref)
        put(2 - got, two_ref, one_other_ref)

    @pl.when(sector == 0)
    def _():
        high[0] = jnp.zeros(high.shape[1:], high.dtype)
        low[0] = jnp.zeros(low.shape[1:], low.dtype)

    @pl.when(sector == lax.axis_size("sec") - 1)
    def _():
        high[2] = jnp.zeros(high.shape[1:], high.dtype)
        low[2] = jnp.zeros(low.shape[1:], low.dtype)

    send_ref[...] = half_product(1 - core, shift_ref, high, low, left_ref, right_ref)


def keep_kernel(shift_ref, left_ref, right_ref, high, low, *refs):
    refs[-1][...] = half_product(core_index(), shift_ref, high, low, left_ref, right_ref)


def product_options(left):
    terms, _, block, _ = left.shape
    return dict(
        mib=16,
        cost_estimate=pl.CostEstimate(
            flops=30 * terms * block**3, bytes_accessed=8 * left.size, transcendentals=0
        ),
    )


def product_to_send(shift, left, right, *arrays, raw=False):
    block = left.shape[-1]
    arrays = [shift, left, right, *arrays]
    return call(
        lambda *refs: send_kernel(raw, *refs),
        [f32(block // 2, block)] + [jax.ShapeDtypeStruct((3, block, block), jnp.bfloat16)] * 2,
        [VMEM] * len(arrays),
        *arrays,
        **product_options(left),
    )


def product_to_keep(shift, left, right, high, low, *after):
    block = left.shape[-1]
    arrays = [shift, left, right, high, low, *after]
    return call(
        keep_kernel, f32(block // 2, block), [VMEM] * len(arrays), *arrays, **product_options(left)
    )


def tile_kernel(first_ref, first_other_ref, field_ref, field_other_ref, out_ref):
    first = jnp.concatenate([first_ref[...], first_other_ref[...]])
    field = jnp.concatenate([field_ref[...], field_other_ref[...]])
    cross, square = total_of(field * first), total_of(field * field)
    theta = jnp.where(square > 0, cross / jnp.where(square > 0, square, 1.0), 0.0)
    resid = first - theta * field
    energy = total_of(resid * resid)
    row = lax.broadcasted_iota(jnp.int32, out_ref.shape, 0)
    lane = lax.broadcasted_iota(jnp.int32, out_ref.shape, 1)
    values = jnp.where(row == 0, cross, jnp.where(row == 1, square, jnp.where(row == 2, energy, 0.0)))
    out_ref[...] = jnp.where(lane == lax.axis_index("sec"), values, 0.0)


def added_kernel(a_ref, b_ref, after_ref, out_ref):
    out_ref[...] = a_ref[...] + b_ref[...]


def merged_kernel(cells, sums_ref, got_ref, out_ref):
    sums = sums_ref[...] + got_ref[...]
    crosses, squares, energies = (sums[i : i + 1] for i in range(3))
    theta = jnp.sum(crosses, axis=1, keepdims=True) / jnp.sum(squares, axis=1, keepdims=True)
    thetas = jnp.where(squares > 0, crosses / jnp.where(squares > 0, squares, 1.0), 0.0)
    energy = jnp.sum(energies + (thetas - theta) ** 2 * squares, axis=1, keepdims=True)
    scale = lax.rsqrt(energy / cells + 1e-06)
    row = lax.broadcasted_iota(jnp.int32, out_ref.shape, 0)
    out_ref[...] = jnp.where(row == 0, theta, scale)


def image_kernel(merged_ref, total_ref, peer_ref, mask_ref, first_ref, out_ref):
    theta, scale = merged_ref[0:1, :], merged_ref[1:2, :]
    total = (total_ref[...] + peer_ref[...]) * mask_ref[...]
    out_ref[...] = scale * (total - theta * first_ref[...])


def correction_kernel(merged_ref, first_ref, first_other_ref, field_ref, field_other_ref, out_ref):
    half = first_ref.shape[0]
    core = core_index()
    theta, scale = merged_ref[0:1, :], merged_ref[1:2, :]
    out_ref[0, rows_of(core, half)] = scale * (first_ref[...] - theta * field_ref[...])
    out_ref[0, rows_of(1 - core, half)] = scale * (first_other_ref[...] - theta * field_other_ref[...])


def output_kernel(mine_ref, other_ref, out_ref):
    half = mine_ref.shape[0]
    core = core_index()
    out_ref[0, rows_of(core, half)] = mine_ref[...]
    out_ref[0, rows_of(1 - core, half)] = other_ref[...]


def local(state, left_ops, right_ops, term_shift, sector_rows, sector_cols):
    sectors, ops = lax.axis_size("sec"), lax.axis_size("op")
    block = state.shape[1]
    half = block // 2

    others = [(i, i ^ 1) for i in range(ops)]
    pairs = [(s, s ^ 1) for s in range(sectors)]
    between = []
    for a in range(ops):
        between += [(s * ops + a, s * ops + (a ^ 2)) for s in (0, sectors - 1)]
        for s in range(1, sectors - 1, 2):
            between += [(s * ops + a, (s + 1) * ops + a), ((s + 1) * ops + a, s * ops + a)]

    def swapped(v):
        return lax.ppermute(v, "op", others)

    def over_chips(total):
        step = 2
        while step < ops // 2:
            total = total + lax.ppermute(total, "op", [(i, i ^ step) for i in range(ops)])
            step *= 2
        return total, lax.ppermute(total, "op", [(i, i ^ step) for i in range(ops)])

    crossing = [(s * ops + a, (s ^ 1) * ops + a) for s in range(sectors) for a in range(1, ops, 2)]
    crossing += [(source, target) for source, target in between if source % 2 == 0]
    crossing_too = [(s * ops + a, (s ^ 1) * ops + a) for s in range(sectors) for a in range(0, ops, 2)]
    crossing_too += [(source, target) for source, target in between if source % 2]
    got = lax.ppermute(state[0], ("sec", "op"), crossing)
    field, field_other, mask, live = call(
        field_kernel,
        [f32(half, block)] * 3 + [jax.ShapeDtypeStruct((8, 128), jnp.int32)],
        [HBM] * 2,
        in_hbm(state), jnp.concatenate([sector_rows, sector_cols]),
        scratch_shapes=[
            pltpu.VMEM((1, block, block), jnp.float32),
            pltpu.SMEM((2,), jnp.int32),
            pltpu.SemaphoreType.DMA((2,)),
        ],
    )
    live = lax.ppermute(live, ("sec", "op"), crossing)
    left, right, shift = load(left_ops, right_ops, term_shift, field)
    got, left, right, live = lax.optimization_barrier((got, left, right, live))
    send, *parts = product_to_send(
        shift, left, right, field, field_other, got, swapped(got), live, swapped(live), raw=True
    )
    total, peer = over_chips(product_to_keep(shift, left, right, *parts) + swapped(send))

    first = (total + peer) * mask
    one = lax.ppermute(first, ("sec", "op"), crossing)
    two = lax.ppermute(first, ("sec", "op"), crossing_too)
    first_other = swapped(first)
    sums = call(tile_kernel, f32(EXTRA, block), [VMEM] * 4, first, first_other, field, field_other)

    def with_distant(sums, step):
        return sums + lax.ppermute(sums, "sec", [(s, s ^ step) for s in range(sectors)])

    step = sectors // 2
    while step > 2:
        sums = with_distant(sums, step)
        step //= 2
    two, sums = lax.optimization_barrier((two, sums))
    send, *parts = product_to_send(
        shift, left, right, first, first_other, one, swapped(one), two, swapped(two)
    )
    sums = call(
        added_kernel,
        f32(EXTRA, block),
        [VMEM] * 3,
        sums, lax.ppermute(sums, "sec", [(s, s ^ 2) for s in range(sectors)]), send,
    )
    keep = product_to_keep(shift, left, right, *parts, sums)
    total, peer = over_chips(keep + swapped(send))

    cells = sectors * block * block
    merged = call(
        lambda *refs: merged_kernel(cells, *refs),
        f32(EXTRA, block),
        [VMEM] * 2,
        sums, lax.ppermute(sums, "sec", pairs),
    )
    image = call(image_kernel, f32(half, block), [VMEM] * 5, merged, total, peer, mask, first)
    correction = call(
        correction_kernel,
        f32(1, block, block),
        [VMEM] * 5,
        merged, first, first_other, field, field_other,
    )
    image = call(output_kernel, f32(1, block, block), [VMEM] * 2, image, swapped(image))
    return correction, image


def solution(mesh):
    in_specs = (
        P("sec", None, None),
        P("op", "sec", None, None),
        P("op", "sec", None, None),
        P("op"),
        P("sec"),
        P("sec"),
    )
    out_specs = (P("sec", None, None), P("sec", None, None))
    return jax.shard_map(local, mesh=mesh, in_specs=in_specs, out_specs=out_specs, check_vma=False)
```

```python
import jax
import jax.numpy as jnp
from jax import lax
from jax.experimental import pallas as pl
from jax.experimental.pallas import tpu as pltpu
from jax.sharding import PartitionSpec as P

EXTRA = 8
VMEM = pl.BlockSpec(memory_space=pltpu.VMEM)
HBM = pl.BlockSpec(memory_space=pltpu.HBM)


def f32(*shape):
    return jax.ShapeDtypeStruct(shape, jnp.float32)


def in_hbm(x):
    return pltpu.with_memory_space_constraint(x, pltpu.HBM)


def call(kernel, out_shape, in_specs, *arrays, mib=4, **options):
    return pl.pallas_call(
        kernel,
        out_shape=out_shape,
        in_specs=in_specs,
        out_specs=jax.tree.map(lambda _: VMEM, out_shape),
        compiler_params=pltpu.CompilerParams(vmem_limit_bytes=mib * 1024 * 1024),
        **options,
    )(*arrays)


def core_index():
    return lax.rem(lax.axis_index("op"), 2)


def rows_of(core, half):
    return pl.ds(pl.multiple_of(core * half, half), half)


def split(x):
    high = x.astype(jnp.bfloat16)
    low = (x - high.astype(jnp.float32)).astype(jnp.bfloat16)
    return high, low


def dot(a, b):
    return jnp.dot(a, b, preferred_element_type=jnp.float32)


def total_of(x):
    return jnp.sum(jnp.sum(x, axis=0, keepdims=True), axis=1, keepdims=True)


def inside(shape, first_row, rows, cols):
    row = lax.broadcasted_iota(jnp.int32, shape, 0) + first_row
    return (row < rows) & (lax.broadcasted_iota(jnp.int32, shape, 1) < cols)


def field_kernel(state_ref, live_ref, field_ref, other_ref, mask_ref, mask_other_ref, live_out, state, live, sems):
    copies = [
        pltpu.make_async_copy(ref, buffer, sems.at[i])
        for i, (ref, buffer) in enumerate(((state_ref, state), (live_ref, live)))
    ]
    for copy in copies:
        copy.start()
    for copy in copies:
        copy.wait()
    half = mask_ref.shape[0]
    core = core_index()
    rows, cols = live[0], live[1]
    for which, ref in ((core, field_ref), (1 - core, other_ref)):
        start = which * half
        ref[...] = jnp.where(inside(ref.shape, start, rows, cols), state[0, rows_of(which, half)], 0.0)
    for which, ref in ((core, mask_ref), (1 - core, mask_other_ref)):
        ref[...] = jnp.where(inside(ref.shape, which * half, rows, cols), 1.0, 0.0)
    row = lax.broadcasted_iota(jnp.int32, live_out.shape, 0)
    live_out[...] = jnp.where(row == 0, rows, cols)


def load_kernel(left_ref, right_ref, shift_ref, field_ref, left_out, right_out, shift_out, right, shift, sems):
    terms = left_ref.shape[0]
    shifts = pltpu.make_async_copy(shift_ref, shift, sems.at[2, 0])
    rights = [
        pltpu.make_async_copy(right_ref.at[term], right.at[term], sems.at[0, term])
        for term in range(terms)
    ]
    lefts = [
        pltpu.make_async_copy(left_ref.at[term], left_out.at[term], sems.at[1, term])
        for term in range(terms)
    ]
    for copy in (shifts, *rights, *lefts):
        copy.start()
    shifts.wait()
    for term in range(terms):
        shift_out[term] = jnp.full(shift_out.shape[1:], shift[term], jnp.int32)
    for term in range(terms):
        rights[term].wait()
        right_out[term, 0] = right[term, 0].T
    for copy in lefts:
        copy.wait()


def load(left_ops, right_ops, shift, field):
    terms = shift.shape[0]
    return call(
        load_kernel,
        [f32(*left_ops.shape), f32(*right_ops.shape), jax.ShapeDtypeStruct((terms, 8, 128), jnp.int32)],
        [HBM, HBM, HBM, VMEM],
        in_hbm(left_ops), in_hbm(right_ops), in_hbm(shift), field,
        mib=8,
        scratch_shapes=[
            pltpu.VMEM(right_ops.shape, jnp.float32),
            pltpu.SMEM(shift.shape, jnp.int32),
            pltpu.SemaphoreType.DMA((3, terms)),
        ],
        cost_estimate=pl.CostEstimate(flops=0, bytes_accessed=8 * left_ops.size, transcendentals=0),
    )


def live_kernel(block_ref, live_ref, out_ref):
    live = inside(block_ref.shape, 0, live_ref[:1, :1], live_ref[1:2, :1])
    out_ref[...] = jnp.where(live, block_ref[...], 0.0)


def half_product(which, shift_ref, high, low, left_ref, right_ref):
    half = left_ref.shape[2] // 2
    rows = rows_of(which, half)

    def thrice(a, b):
        (a_high, a_low), (b_high, b_low) = a, b
        both = dot(jnp.concatenate([a_high, a_low]), b_high)
        return both[:half] + (both[half:] + dot(a_high, b_low))

    inner = []
    for term in range(left_ref.shape[0]):
        source = 1 - shift_ref[term][0, 0]
        inner.append(thrice(split(left_ref[term, 0, rows]), (high[source], low[source])))
    out = None
    for term in range(right_ref.shape[0]):
        part = thrice(split(inner[term]), split(right_ref[term, 0]))
        out = part if out is None else out + part
    return out


def send_kernel(raw, shift_ref, left_ref, right_ref, own_ref, own_other_ref, *refs):
    *refs, send_ref, high, low = refs
    half, block = send_ref.shape
    core, sector = core_index(), lax.axis_index("sec")
    slot = jnp.where(lax.rem(sector, 2) == 0, 2, 0)
    got = jnp.where(core == 1, slot, 2 - slot)

    def put(index, mine_ref, other_ref):
        for which, ref in ((core, mine_ref), (1 - core, other_ref)):
            rows = rows_of(which, half)
            high[index, rows], low[index, rows] = split(ref[...])

    put(1, own_ref, own_other_ref)
    if raw:
        for index, ref in zip((got, 2 - got), refs):
            high[index], low[index] = split(ref[...])
    else:
        one_ref, one_other_ref, two_ref, two_other_ref = refs
        put(got, one_ref, two_other_ref)
        put(2 - got, two_ref, one_other_ref)

    @pl.when(sector == 0)
    def _():
        high[0] = jnp.zeros(high.shape[1:], high.dtype)
        low[0] = jnp.zeros(low.shape[1:], low.dtype)

    @pl.when(sector == lax.axis_size("sec") - 1)
    def _():
        high[2] = jnp.zeros(high.shape[1:], high.dtype)
        low[2] = jnp.zeros(low.shape[1:], low.dtype)

    send_ref[...] = half_product(1 - core, shift_ref, high, low, left_ref, right_ref)


def keep_kernel(shift_ref, left_ref, right_ref, high, low, *refs):
    refs[-1][...] = half_product(core_index(), shift_ref, high, low, left_ref, right_ref)


def product_options(left, count=30):
    terms, _, block, _ = left.shape
    return dict(
        mib=16,
        cost_estimate=pl.CostEstimate(
            flops=count * terms * block**3, bytes_accessed=8 * left.size, transcendentals=0
        ),
    )


def product_to_send(shift, left, right, *arrays, raw=False):
    block = left.shape[-1]
    arrays = [shift, left, right, *arrays]
    return call(
        lambda *refs: send_kernel(raw, *refs),
        [f32(block // 2, block)] + [jax.ShapeDtypeStruct((3, block, block), jnp.bfloat16)] * 2,
        [VMEM] * len(arrays),
        *arrays,
        **product_options(left),
    )


def product_to_keep(shift, left, right, high, low, *after):
    block = left.shape[-1]
    arrays = [shift, left, right, high, low, *after]
    return call(
        keep_kernel, f32(block // 2, block), [VMEM] * len(arrays), *arrays, **product_options(left, 1)
    )


def tile_kernel(first_ref, first_other_ref, field_ref, field_other_ref, out_ref):
    first = jnp.concatenate([first_ref[...], first_other_ref[...]])
    field = jnp.concatenate([field_ref[...], field_other_ref[...]])
    cross, square = total_of(field * first), total_of(field * field)
    theta = jnp.where(square > 0, cross / jnp.where(square > 0, square, 1.0), 0.0)
    resid = first - theta * field
    energy = total_of(resid * resid)
    row = lax.broadcasted_iota(jnp.int32, out_ref.shape, 0)
    lane = lax.broadcasted_iota(jnp.int32, out_ref.shape, 1)
    values = jnp.where(row == 0, cross, jnp.where(row == 1, square, jnp.where(row == 2, energy, 0.0)))
    out_ref[...] = jnp.where(lane == lax.axis_index("sec"), values, 0.0)


def added_after_kernel(a_ref, b_ref, after_ref, out_ref):
    out_ref[...] = a_ref[...] + b_ref[...]


def added_kernel(a_ref, b_ref, after_ref, out_ref):
    out_ref[...] = a_ref[...] + b_ref[...]


def merged_kernel(cells, sums_ref, got_ref, out_ref):
    sums = sums_ref[...] + got_ref[...]
    crosses, squares, energies = (sums[i : i + 1] for i in range(3))
    theta = jnp.sum(crosses, axis=1, keepdims=True) / jnp.sum(squares, axis=1, keepdims=True)
    thetas = jnp.where(squares > 0, crosses / jnp.where(squares > 0, squares, 1.0), 0.0)
    energy = jnp.sum(energies + (thetas - theta) ** 2 * squares, axis=1, keepdims=True)
    scale = lax.rsqrt(energy / cells + 1e-06)
    row = lax.broadcasted_iota(jnp.int32, out_ref.shape, 0)
    out_ref[...] = jnp.where(row == 0, theta, scale)


def correction_kernel(merged_ref, first_ref, first_other_ref, field_ref, field_other_ref, out_ref):
    half = first_ref.shape[0]
    core = core_index()
    theta, scale = merged_ref[0:1, :], merged_ref[1:2, :]
    out_ref[0, rows_of(core, half)] = scale * (first_ref[...] - theta * field_ref[...])
    out_ref[0, rows_of(1 - core, half)] = scale * (first_other_ref[...] - theta * field_other_ref[...])


def image_kernel(merged_ref, *refs):
    *refs, out_ref = refs
    half = refs[0].shape[0]
    core = core_index()
    theta, scale = merged_ref[0:1, :], merged_ref[1:2, :]
    for which, (total, peer, mask, first) in ((core, refs[:4]), (1 - core, refs[4:])):
        product = (total[...] + peer[...]) * mask[...]
        out_ref[0, rows_of(which, half)] = scale * (product - theta * first[...])


def local(state, left_ops, right_ops, term_shift, sector_rows, sector_cols):
    sectors, ops = lax.axis_size("sec"), lax.axis_size("op")
    block = state.shape[1]
    half = block // 2

    others = [(i, i ^ 1) for i in range(ops)]
    pairs = [(s, s ^ 1) for s in range(sectors)]
    between = []
    for a in range(ops):
        between += [(s * ops + a, s * ops + (a ^ 2)) for s in (0, sectors - 1)]
        for s in range(1, sectors - 1, 2):
            between += [(s * ops + a, (s + 1) * ops + a), ((s + 1) * ops + a, s * ops + a)]

    def swapped(v):
        return lax.ppermute(v, "op", others)

    def over_chips(total):
        step = 2
        while step < ops // 2:
            total = total + lax.ppermute(total, "op", [(i, i ^ step) for i in range(ops)])
            step *= 2
        return total, lax.ppermute(total, "op", [(i, i ^ step) for i in range(ops)])

    crossing = [(s * ops + a, (s ^ 1) * ops + a) for s in range(sectors) for a in range(1, ops, 2)]
    crossing += [(source, target) for source, target in between if source % 2 == 0]
    crossing_too = [(s * ops + a, (s ^ 1) * ops + a) for s in range(sectors) for a in range(0, ops, 2)]
    crossing_too += [(source, target) for source, target in between if source % 2]
    got = lax.ppermute(state[0], ("sec", "op"), crossing)
    field, field_other, mask, mask_other, live = call(
        field_kernel,
        [f32(half, block)] * 4 + [jax.ShapeDtypeStruct((8, 128), jnp.int32)],
        [HBM] * 2,
        in_hbm(state), jnp.concatenate([sector_rows, sector_cols]),
        scratch_shapes=[
            pltpu.VMEM((1, block, block), jnp.float32),
            pltpu.SMEM((2,), jnp.int32),
            pltpu.SemaphoreType.DMA((2,)),
        ],
    )
    live = lax.ppermute(live, ("sec", "op"), crossing)
    left, right, shift = load(left_ops, right_ops, term_shift, field)
    got, left, right, live = lax.optimization_barrier((got, left, right, live))
    got = call(live_kernel, f32(block, block), [VMEM] * 2, got, live)
    send, *parts = product_to_send(
        shift, left, right, field, field_other, got, swapped(got), raw=True
    )
    total, peer = over_chips(product_to_keep(shift, left, right, *parts) + swapped(send))

    first = (total + peer) * mask
    one = lax.ppermute(first, ("sec", "op"), crossing)
    two = lax.ppermute(first, ("sec", "op"), crossing_too)
    first_other = swapped(first)
    sums = call(tile_kernel, f32(EXTRA, block), [VMEM] * 4, first, first_other, field, field_other)

    def with_distant(sums, step):
        return sums + lax.ppermute(sums, "sec", [(s, s ^ step) for s in range(sectors)])

    step = sectors // 2
    while step > 2:
        sums = with_distant(sums, step)
        step //= 2
    two, sums = lax.optimization_barrier((two, sums))
    send, *parts = product_to_send(
        shift, left, right, first, first_other, one, swapped(one), two, swapped(two)
    )
    keep = product_to_keep(shift, left, right, *parts)
    sums = call(
        added_kernel,
        f32(EXTRA, block),
        [VMEM] * 3,
        sums, lax.ppermute(sums, "sec", [(s, s ^ 2) for s in range(sectors)]), keep,
        cost_estimate=pl.CostEstimate(flops=10**10, bytes_accessed=0, transcendentals=0),
    )
    total, peer = over_chips(
        call(added_after_kernel, f32(half, block), [VMEM] * 3, keep, swapped(send), sums)
    )

    pair_sums = lax.ppermute(sums, "sec", pairs)
    peer, pair_sums = lax.optimization_barrier((peer, pair_sums))
    cells = sectors * block * block
    merged = call(
        lambda *refs: merged_kernel(cells, *refs),
        f32(EXTRA, block),
        [VMEM] * 2,
        sums, pair_sums,
    )
    correction = call(
        correction_kernel,
        f32(1, block, block),
        [VMEM] * 5,
        merged, first, first_other, field, field_other,
    )
    image = call(
        image_kernel,
        f32(1, block, block),
        [VMEM] * 9,
        merged, total, peer, mask, first, swapped(total), swapped(peer), mask_other, first_other,
    )
    return correction, image


def solution(mesh):
    in_specs = (
        P("sec", None, None),
        P("op", "sec", None, None),
        P("op", "sec", None, None),
        P("op"),
        P("sec"),
        P("sec"),
    )
    out_specs = (P("sec", None, None), P("sec", None, None))
    return jax.shard_map(local, mesh=mesh, in_specs=in_specs, out_specs=out_specs, check_vma=False)
```

```python
import jax
import jax.numpy as jnp
from jax import lax
from jax.experimental import pallas as pl
from jax.experimental.pallas import tpu as pltpu
from jax.sharding import PartitionSpec as P

EXTRA = 8
VMEM = pl.BlockSpec(memory_space=pltpu.VMEM)
HBM = pl.BlockSpec(memory_space=pltpu.HBM)


def f32(*shape):
    return jax.ShapeDtypeStruct(shape, jnp.float32)


def in_hbm(x):
    return pltpu.with_memory_space_constraint(x, pltpu.HBM)


def call(kernel, out_shape, in_specs, *arrays, mib=4, **options):
    return pl.pallas_call(
        kernel,
        out_shape=out_shape,
        in_specs=in_specs,
        out_specs=jax.tree.map(lambda _: VMEM, out_shape),
        compiler_params=pltpu.CompilerParams(vmem_limit_bytes=mib * 1024 * 1024),
        **options,
    )(*arrays)


def core_index():
    return lax.rem(lax.axis_index("op"), 2)


def rows_of(core, half):
    return pl.ds(pl.multiple_of(core * half, half), half)


def split(x):
    high = x.astype(jnp.bfloat16)
    low = (x - high.astype(jnp.float32)).astype(jnp.bfloat16)
    return high, low


def dot(a, b):
    return jnp.dot(a, b, preferred_element_type=jnp.float32)


def total_of(x):
    return jnp.sum(jnp.sum(x, axis=0, keepdims=True), axis=1, keepdims=True)


def inside(shape, first_row, rows, cols):
    row = lax.broadcasted_iota(jnp.int32, shape, 0) + first_row
    return (row < rows) & (lax.broadcasted_iota(jnp.int32, shape, 1) < cols)


def field_kernel(state_ref, live_ref, field_ref, other_ref, mask_ref, live_out, state, live, sems):
    copies = [
        pltpu.make_async_copy(ref, buffer, sems.at[i])
        for i, (ref, buffer) in enumerate(((state_ref, state), (live_ref, live)))
    ]
    for copy in copies:
        copy.start()
    for copy in copies:
        copy.wait()
    half = mask_ref.shape[0]
    core = core_index()
    rows, cols = live[0], live[1]
    for which, ref in ((core, field_ref), (1 - core, other_ref)):
        start = which * half
        ref[...] = jnp.where(inside(ref.shape, start, rows, cols), state[0, rows_of(which, half)], 0.0)
    mask_ref[...] = jnp.where(inside(mask_ref.shape, core * half, rows, cols), 1.0, 0.0)
    row = lax.broadcasted_iota(jnp.int32, live_out.shape, 0)
    live_out[...] = jnp.where(row == 0, rows, cols)


def load_kernel(left_ref, right_ref, shift_ref, field_ref, left_out, right_out, shift_out, right, shift, sems):
    terms = left_ref.shape[0]
    shifts = pltpu.make_async_copy(shift_ref, shift, sems.at[2, 0])
    rights = [
        pltpu.make_async_copy(right_ref.at[term], right.at[term], sems.at[0, term])
        for term in range(terms)
    ]
    lefts = [
        pltpu.make_async_copy(left_ref.at[term], left_out.at[term], sems.at[1, term])
        for term in range(terms)
    ]
    for copy in (shifts, *rights, *lefts):
        copy.start()
    shifts.wait()
    for term in range(terms):
        shift_out[term] = jnp.full(shift_out.shape[1:], shift[term], jnp.int32)
    for term in range(terms):
        rights[term].wait()
        right_out[term, 0] = right[term, 0].T
    for copy in lefts:
        copy.wait()


def load(left_ops, right_ops, shift, field):
    terms = shift.shape[0]
    return call(
        load_kernel,
        [f32(*left_ops.shape), f32(*right_ops.shape), jax.ShapeDtypeStruct((terms, 8, 128), jnp.int32)],
        [HBM, HBM, HBM, VMEM],
        in_hbm(left_ops), in_hbm(right_ops), in_hbm(shift), field,
        mib=8,
        scratch_shapes=[
            pltpu.VMEM(right_ops.shape, jnp.float32),
            pltpu.SMEM(shift.shape, jnp.int32),
            pltpu.SemaphoreType.DMA((3, terms)),
        ],
        cost_estimate=pl.CostEstimate(flops=0, bytes_accessed=8 * left_ops.size, transcendentals=0),
    )


def half_product(which, shift_ref, high, low, left_ref, right_ref):
    half = left_ref.shape[2] // 2
    rows = rows_of(which, half)

    def thrice(a, b):
        (a_high, a_low), (b_high, b_low) = a, b
        both = dot(jnp.concatenate([a_high, a_low]), b_high)
        return both[:half] + (both[half:] + dot(a_high, b_low))

    inner = []
    for term in range(left_ref.shape[0]):
        source = 1 - shift_ref[term][0, 0]
        inner.append(thrice(split(left_ref[term, 0, rows]), (high[source], low[source])))
    out = None
    for term in range(right_ref.shape[0]):
        part = thrice(split(inner[term]), split(right_ref[term, 0]))
        out = part if out is None else out + part
    return out


def send_kernel(raw, shift_ref, left_ref, right_ref, own_ref, own_other_ref, *refs):
    *refs, send_ref, high, low = refs
    half, block = send_ref.shape
    core, sector = core_index(), lax.axis_index("sec")
    slot = jnp.where(lax.rem(sector, 2) == 0, 2, 0)
    got = jnp.where(core == 1, slot, 2 - slot)

    def is_beyond(slot):
        last = lax.axis_size("sec") - 1
        return ((sector == 0) & (slot == 0)) | ((sector == last) & (slot == 2))

    def put(index, mine_ref, other_ref):
        for which, ref in ((core, mine_ref), (1 - core, other_ref)):
            rows = rows_of(which, half)
            high[index, rows], low[index, rows] = split(jnp.where(is_beyond(index), 0.0, ref[...]))

    for which, ref in ((core, own_ref), (1 - core, own_other_ref)):
        rows = rows_of(which, half)
        high[1, rows], low[1, rows] = split(ref[...])
    if raw:
        for index, ref, live_ref in zip((got, 2 - got), refs[:2], refs[2:]):
            rows = jnp.where(is_beyond(index), 0, live_ref[:1, :1])
            live = inside((block, block), 0, rows, live_ref[1:2, :1])
            high[index], low[index] = split(jnp.where(live, ref[...], 0.0))
    else:
        one_ref, one_other_ref, two_ref, two_other_ref = refs
        put(got, one_ref, two_other_ref)
        put(2 - got, two_ref, one_other_ref)

    send_ref[...] = half_product(1 - core, shift_ref, high, low, left_ref, right_ref)


def keep_kernel(shift_ref, left_ref, right_ref, high, low, *refs):
    refs[-1][...] = half_product(core_index(), shift_ref, high, low, left_ref, right_ref)


def product_options(left):
    terms, _, block, _ = left.shape
    return dict(
        mib=16,
        cost_estimate=pl.CostEstimate(
            flops=30 * terms * block**3, bytes_accessed=8 * left.size, transcendentals=0
        ),
    )


def product_to_send(shift, left, right, *arrays, raw=False):
    block = left.shape[-1]
    arrays = [shift, left, right, *arrays]
    return call(
        lambda *refs: send_kernel(raw, *refs),
        [f32(block // 2, block)] + [jax.ShapeDtypeStruct((3, block, block), jnp.bfloat16)] * 2,
        [VMEM] * len(arrays),
        *arrays,
        **product_options(left),
    )


def product_to_keep(shift, left, right, high, low, *after):
    block = left.shape[-1]
    arrays = [shift, left, right, high, low, *after]
    return call(
        keep_kernel, f32(block // 2, block), [VMEM] * len(arrays), *arrays, **product_options(left)
    )


def tile_kernel(first_ref, first_other_ref, field_ref, field_other_ref, out_ref):
    first = jnp.concatenate([first_ref[...], first_other_ref[...]])
    field = jnp.concatenate([field_ref[...], field_other_ref[...]])
    cross, square = total_of(field * first), total_of(field * field)
    theta = jnp.where(square > 0, cross / jnp.where(square > 0, square, 1.0), 0.0)
    resid = first - theta * field
    energy = total_of(resid * resid)
    row = lax.broadcasted_iota(jnp.int32, out_ref.shape, 0)
    lane = lax.broadcasted_iota(jnp.int32, out_ref.shape, 1)
    values = jnp.where(row == 0, cross, jnp.where(row == 1, square, jnp.where(row == 2, energy, 0.0)))
    out_ref[...] = jnp.where(lane == lax.axis_index("sec"), values, 0.0)


def added_kernel(a_ref, b_ref, after_ref, out_ref):
    out_ref[...] = a_ref[...] + b_ref[...]


def merged_kernel(cells, sums_ref, got_ref, out_ref):
    sums = sums_ref[...] + got_ref[...]
    crosses, squares, energies = (sums[i : i + 1] for i in range(3))
    theta = jnp.sum(crosses, axis=1, keepdims=True) / jnp.sum(squares, axis=1, keepdims=True)
    thetas = jnp.where(squares > 0, crosses / jnp.where(squares > 0, squares, 1.0), 0.0)
    energy = jnp.sum(energies + (thetas - theta) ** 2 * squares, axis=1, keepdims=True)
    scale = lax.rsqrt(energy / cells + 1e-06)
    row = lax.broadcasted_iota(jnp.int32, out_ref.shape, 0)
    out_ref[...] = jnp.where(row == 0, theta, scale)


def image_kernel(merged_ref, total_ref, peer_ref, mask_ref, first_ref, out_ref):
    theta, scale = merged_ref[0:1, :], merged_ref[1:2, :]
    total = (total_ref[...] + peer_ref[...]) * mask_ref[...]
    out_ref[...] = scale * (total - theta * first_ref[...])


def correction_kernel(merged_ref, first_ref, first_other_ref, field_ref, field_other_ref, out_ref):
    half = first_ref.shape[0]
    core = core_index()
    theta, scale = merged_ref[0:1, :], merged_ref[1:2, :]
    out_ref[0, rows_of(core, half)] = scale * (first_ref[...] - theta * field_ref[...])
    out_ref[0, rows_of(1 - core, half)] = scale * (first_other_ref[...] - theta * field_other_ref[...])


def output_kernel(mine_ref, other_ref, out_ref):
    half = mine_ref.shape[0]
    core = core_index()
    out_ref[0, rows_of(core, half)] = mine_ref[...]
    out_ref[0, rows_of(1 - core, half)] = other_ref[...]


def local(state, left_ops, right_ops, term_shift, sector_rows, sector_cols):
    sectors, ops = lax.axis_size("sec"), lax.axis_size("op")
    block = state.shape[1]
    half = block // 2

    others = [(i, i ^ 1) for i in range(ops)]
    pairs = [(s, s ^ 1) for s in range(sectors)]
    between = []
    for a in range(ops):
        between += [(s * ops + a, s * ops + (a ^ 2)) for s in (0, sectors - 1)]
        for s in range(1, sectors - 1, 2):
            between += [(s * ops + a, (s + 1) * ops + a), ((s + 1) * ops + a, s * ops + a)]

    def swapped(v):
        return lax.ppermute(v, "op", others)

    def over_chips(total):
        step = 2
        while step < ops // 2:
            total = total + lax.ppermute(total, "op", [(i, i ^ step) for i in range(ops)])
            step *= 2
        return total, lax.ppermute(total, "op", [(i, i ^ step) for i in range(ops)])

    crossing = [(s * ops + a, (s ^ 1) * ops + a) for s in range(sectors) for a in range(1, ops, 2)]
    crossing += [(source, target) for source, target in between if source % 2 == 0]
    crossing_too = [(s * ops + a, (s ^ 1) * ops + a) for s in range(sectors) for a in range(0, ops, 2)]
    crossing_too += [(source, target) for source, target in between if source % 2]
    got = lax.ppermute(state[0], ("sec", "op"), crossing)
    field, field_other, mask, live = call(
        field_kernel,
        [f32(half, block)] * 3 + [jax.ShapeDtypeStruct((8, 128), jnp.int32)],
        [HBM] * 2,
        in_hbm(state), jnp.concatenate([sector_rows, sector_cols]),
        scratch_shapes=[
            pltpu.VMEM((1, block, block), jnp.float32),
            pltpu.SMEM((2,), jnp.int32),
            pltpu.SemaphoreType.DMA((2,)),
        ],
    )
    live = lax.ppermute(live, ("sec", "op"), crossing)
    left, right, shift = load(left_ops, right_ops, term_shift, field)
    got, left, right, live = lax.optimization_barrier((got, left, right, live))
    send, *parts = product_to_send(
        shift, left, right, field, field_other, got, swapped(got), live, swapped(live), raw=True
    )
    total, peer = over_chips(product_to_keep(shift, left, right, *parts) + swapped(send))

    first = (total + peer) * mask
    one = lax.ppermute(first, ("sec", "op"), crossing)
    two = lax.ppermute(first, ("sec", "op"), crossing_too)
    first_other = swapped(first)
    sums = call(tile_kernel, f32(EXTRA, block), [VMEM] * 4, first, first_other, field, field_other)

    def with_distant(sums, step):
        return sums + lax.ppermute(sums, "sec", [(s, s ^ step) for s in range(sectors)])

    step = sectors // 2
    while step > 2:
        sums = with_distant(sums, step)
        step //= 2
    two, sums = lax.optimization_barrier((two, sums))
    send, *parts = product_to_send(
        shift, left, right, first, first_other, one, swapped(one), two, swapped(two)
    )
    sums = call(
        added_kernel,
        f32(EXTRA, block),
        [VMEM] * 3,
        sums, lax.ppermute(sums, "sec", [(s, s ^ 2) for s in range(sectors)]), send,
    )
    keep = product_to_keep(shift, left, right, *parts, sums)
    total, peer = over_chips(keep + swapped(send))

    cells = sectors * block * block
    merged = call(
        lambda *refs: merged_kernel(cells, *refs),
        f32(EXTRA, block),
        [VMEM] * 2,
        sums, lax.ppermute(sums, "sec", pairs),
    )
    image = call(image_kernel, f32(half, block), [VMEM] * 5, merged, total, peer, mask, first)
    correction = call(
        correction_kernel,
        f32(1, block, block),
        [VMEM] * 5,
        merged, first, first_other, field, field_other,
    )
    image = call(output_kernel, f32(1, block, block), [VMEM] * 2, image, swapped(image))
    return correction, image


def solution(mesh):
    in_specs = (
        P("sec", None, None),
        P("op", "sec", None, None),
        P("op", "sec", None, None),
        P("op"),
        P("sec"),
        P("sec"),
    )
    out_specs = (P("sec", None, None), P("sec", None, None))
    return jax.shard_map(local, mesh=mesh, in_specs=in_specs, out_specs=out_specs, check_vma=False)
```

```python
import jax
import jax.numpy as jnp
from jax import lax
from jax.experimental import pallas as pl
from jax.experimental.pallas import tpu as pltpu
from jax.sharding import PartitionSpec as P

EXTRA = 8
VMEM = pl.BlockSpec(memory_space=pltpu.VMEM)
HBM = pl.BlockSpec(memory_space=pltpu.HBM)


def f32(*shape):
    return jax.ShapeDtypeStruct(shape, jnp.float32)


def in_hbm(x):
    return pltpu.with_memory_space_constraint(x, pltpu.HBM)


def call(kernel, out_shape, in_specs, *arrays, mib=4, **options):
    return pl.pallas_call(
        kernel,
        out_shape=out_shape,
        in_specs=in_specs,
        out_specs=jax.tree.map(lambda _: VMEM, out_shape),
        compiler_params=pltpu.CompilerParams(vmem_limit_bytes=mib * 1024 * 1024),
        **options,
    )(*arrays)


def core_index():
    return lax.rem(lax.axis_index("op"), 2)


def rows_of(core, half):
    return pl.ds(pl.multiple_of(core * half, half), half)


def split(x):
    high = x.astype(jnp.bfloat16)
    low = (x - high.astype(jnp.float32)).astype(jnp.bfloat16)
    return high, low


def dot(a, b):
    return jnp.dot(a, b, preferred_element_type=jnp.float32)


def total_of(x):
    return jnp.sum(jnp.sum(x, axis=0, keepdims=True), axis=1, keepdims=True)


def inside(shape, first_row, rows, cols):
    row = lax.broadcasted_iota(jnp.int32, shape, 0) + first_row
    return (row < rows) & (lax.broadcasted_iota(jnp.int32, shape, 1) < cols)


def field_kernel(state_ref, live_ref, field_ref, other_ref, mask_ref, mask_other_ref, live_out, state, live, sems):
    copies = [
        pltpu.make_async_copy(ref, buffer, sems.at[i])
        for i, (ref, buffer) in enumerate(((state_ref, state), (live_ref, live)))
    ]
    for copy in copies:
        copy.start()
    for copy in copies:
        copy.wait()
    half = mask_ref.shape[0]
    core = core_index()
    rows, cols = live[0], live[1]
    for which, ref in ((core, field_ref), (1 - core, other_ref)):
        start = which * half
        ref[...] = jnp.where(inside(ref.shape, start, rows, cols), state[0, rows_of(which, half)], 0.0)
    for which, ref in ((core, mask_ref), (1 - core, mask_other_ref)):
        ref[...] = jnp.where(inside(ref.shape, which * half, rows, cols), 1.0, 0.0)
    row = lax.broadcasted_iota(jnp.int32, live_out.shape, 0)
    live_out[...] = jnp.where(row == 0, rows, cols)


def load_kernel(left_ref, right_ref, shift_ref, field_ref, left_out, right_out, shift_out, right, shift, sems):
    terms = left_ref.shape[0]
    shifts = pltpu.make_async_copy(shift_ref, shift, sems.at[2, 0])
    rights = [
        pltpu.make_async_copy(right_ref.at[term], right.at[term], sems.at[0, term])
        for term in range(terms)
    ]
    lefts = [
        pltpu.make_async_copy(left_ref.at[term], left_out.at[term], sems.at[1, term])
        for term in range(terms)
    ]
    for copy in (shifts, *rights, *lefts):
        copy.start()
    shifts.wait()
    for term in range(terms):
        shift_out[term] = jnp.full(shift_out.shape[1:], shift[term], jnp.int32)
    for term in range(terms):
        rights[term].wait()
        right_out[term, 0] = right[term, 0].T
    for copy in lefts:
        copy.wait()


def load(left_ops, right_ops, shift, field):
    terms = shift.shape[0]
    return call(
        load_kernel,
        [f32(*left_ops.shape), f32(*right_ops.shape), jax.ShapeDtypeStruct((terms, 8, 128), jnp.int32)],
        [HBM, HBM, HBM, VMEM],
        in_hbm(left_ops), in_hbm(right_ops), in_hbm(shift), field,
        mib=8,
        scratch_shapes=[
            pltpu.VMEM(right_ops.shape, jnp.float32),
            pltpu.SMEM(shift.shape, jnp.int32),
            pltpu.SemaphoreType.DMA((3, terms)),
        ],
        cost_estimate=pl.CostEstimate(flops=0, bytes_accessed=8 * left_ops.size, transcendentals=0),
    )


def live_kernel(block_ref, live_ref, out_ref):
    live = inside(block_ref.shape, 0, live_ref[:1, :1], live_ref[1:2, :1])
    out_ref[...] = jnp.where(live, block_ref[...], 0.0)


def half_product(which, shift_ref, high, low, left_ref, right_ref):
    half = left_ref.shape[2] // 2
    rows = rows_of(which, half)

    def thrice(a, b):
        (a_high, a_low), (b_high, b_low) = a, b
        both = dot(jnp.concatenate([a_high, a_low]), b_high)
        return both[:half] + (both[half:] + dot(a_high, b_low))

    inner = []
    for term in range(left_ref.shape[0]):
        source = 1 - shift_ref[term][0, 0]
        inner.append(thrice(split(left_ref[term, 0, rows]), (high[source], low[source])))
    out = None
    for term in range(right_ref.shape[0]):
        part = thrice(split(inner[term]), split(right_ref[term, 0]))
        out = part if out is None else out + part
    return out


def send_kernel(raw, shift_ref, left_ref, right_ref, own_ref, own_other_ref, *refs):
    *refs, send_ref, high, low = refs
    half, block = send_ref.shape
    core, sector = core_index(), lax.axis_index("sec")
    slot = jnp.where(lax.rem(sector, 2) == 0, 2, 0)
    got = jnp.where(core == 1, slot, 2 - slot)

    def is_beyond(slot):
        last = lax.axis_size("sec") - 1
        return ((sector == 0) & (slot == 0)) | ((sector == last) & (slot == 2))

    def put(index, mine_ref, other_ref):
        for which, ref in ((core, mine_ref), (1 - core, other_ref)):
            rows = rows_of(which, half)
            high[index, rows], low[index, rows] = split(jnp.where(is_beyond(index), 0.0, ref[...]))

    for which, ref in ((core, own_ref), (1 - core, own_other_ref)):
        rows = rows_of(which, half)
        high[1, rows], low[1, rows] = split(ref[...])
    if raw:
        for index, ref in zip((got, 2 - got), refs):
            high[index], low[index] = split(jnp.where(is_beyond(index), 0.0, ref[...]))
    else:
        one_ref, one_other_ref, two_ref, two_other_ref = refs
        put(got, one_ref, two_other_ref)
        put(2 - got, two_ref, one_other_ref)

    send_ref[...] = half_product(1 - core, shift_ref, high, low, left_ref, right_ref)


def keep_kernel(shift_ref, left_ref, right_ref, high, low, *refs):
    refs[-1][...] = half_product(core_index(), shift_ref, high, low, left_ref, right_ref)


def product_options(left, count=30):
    terms, _, block, _ = left.shape
    return dict(
        mib=16,
        cost_estimate=pl.CostEstimate(
            flops=count * terms * block**3, bytes_accessed=8 * left.size, transcendentals=0
        ),
    )


def product_to_send(shift, left, right, *arrays, raw=False):
    block = left.shape[-1]
    arrays = [shift, left, right, *arrays]
    return call(
        lambda *refs: send_kernel(raw, *refs),
        [f32(block // 2, block)] + [jax.ShapeDtypeStruct((3, block, block), jnp.bfloat16)] * 2,
        [VMEM] * len(arrays),
        *arrays,
        **product_options(left),
    )


def product_to_keep(shift, left, right, high, low, *after):
    block = left.shape[-1]
    arrays = [shift, left, right, high, low, *after]
    return call(
        keep_kernel, f32(block // 2, block), [VMEM] * len(arrays), *arrays, **product_options(left, 1)
    )


def tile_kernel(first_ref, first_other_ref, field_ref, field_other_ref, out_ref):
    first = jnp.concatenate([first_ref[...], first_other_ref[...]])
    field = jnp.concatenate([field_ref[...], field_other_ref[...]])
    cross, square = total_of(field * first), total_of(field * field)
    theta = jnp.where(square > 0, cross / jnp.where(square > 0, square, 1.0), 0.0)
    resid = first - theta * field
    energy = total_of(resid * resid)
    row = lax.broadcasted_iota(jnp.int32, out_ref.shape, 0)
    lane = lax.broadcasted_iota(jnp.int32, out_ref.shape, 1)
    values = jnp.where(row == 0, cross, jnp.where(row == 1, square, jnp.where(row == 2, energy, 0.0)))
    out_ref[...] = jnp.where(lane == lax.axis_index("sec"), values, 0.0)


def added_after_kernel(a_ref, b_ref, after_ref, out_ref):
    out_ref[...] = a_ref[...] + b_ref[...]


def added_kernel(a_ref, b_ref, after_ref, out_ref):
    out_ref[...] = a_ref[...] + b_ref[...]


def merged_kernel(cells, sums_ref, got_ref, out_ref):
    sums = sums_ref[...] + got_ref[...]
    crosses, squares, energies = (sums[i : i + 1] for i in range(3))
    theta = jnp.sum(crosses, axis=1, keepdims=True) / jnp.sum(squares, axis=1, keepdims=True)
    thetas = jnp.where(squares > 0, crosses / jnp.where(squares > 0, squares, 1.0), 0.0)
    energy = jnp.sum(energies + (thetas - theta) ** 2 * squares, axis=1, keepdims=True)
    scale = lax.rsqrt(energy / cells + 1e-06)
    row = lax.broadcasted_iota(jnp.int32, out_ref.shape, 0)
    out_ref[...] = jnp.where(row == 0, theta, scale)


def correction_kernel(merged_ref, first_ref, first_other_ref, field_ref, field_other_ref, out_ref):
    half = first_ref.shape[0]
    core = core_index()
    theta, scale = merged_ref[0:1, :], merged_ref[1:2, :]
    out_ref[0, rows_of(core, half)] = scale * (first_ref[...] - theta * field_ref[...])
    out_ref[0, rows_of(1 - core, half)] = scale * (first_other_ref[...] - theta * field_other_ref[...])


def image_kernel(merged_ref, *refs):
    *refs, out_ref = refs
    half = refs[0].shape[0]
    core = core_index()
    theta, scale = merged_ref[0:1, :], merged_ref[1:2, :]
    for which, (total, peer, mask, first) in ((core, refs[:4]), (1 - core, refs[4:])):
        product = (total[...] + peer[...]) * mask[...]
        out_ref[0, rows_of(which, half)] = scale * (product - theta * first[...])


def local(state, left_ops, right_ops, term_shift, sector_rows, sector_cols):
    sectors, ops = lax.axis_size("sec"), lax.axis_size("op")
    block = state.shape[1]
    half = block // 2

    others = [(i, i ^ 1) for i in range(ops)]
    pairs = [(s, s ^ 1) for s in range(sectors)]
    between = []
    for a in range(ops):
        between += [(s * ops + a, s * ops + (a ^ 2)) for s in (0, sectors - 1)]
        for s in range(1, sectors - 1, 2):
            between += [(s * ops + a, (s + 1) * ops + a), ((s + 1) * ops + a, s * ops + a)]

    def swapped(v):
        return lax.ppermute(v, "op", others)

    def over_chips(total):
        step = 2
        while step < ops // 2:
            total = total + lax.ppermute(total, "op", [(i, i ^ step) for i in range(ops)])
            step *= 2
        return total, lax.ppermute(total, "op", [(i, i ^ step) for i in range(ops)])

    crossing = [(s * ops + a, (s ^ 1) * ops + a) for s in range(sectors) for a in range(1, ops, 2)]
    crossing += [(source, target) for source, target in between if source % 2 == 0]
    crossing_too = [(s * ops + a, (s ^ 1) * ops + a) for s in range(sectors) for a in range(0, ops, 2)]
    crossing_too += [(source, target) for source, target in between if source % 2]
    got = lax.ppermute(state[0], ("sec", "op"), crossing)
    field, field_other, mask, mask_other, live = call(
        field_kernel,
        [f32(half, block)] * 4 + [jax.ShapeDtypeStruct((8, 128), jnp.int32)],
        [HBM] * 2,
        in_hbm(state), jnp.concatenate([sector_rows, sector_cols]),
        scratch_shapes=[
            pltpu.VMEM((1, block, block), jnp.float32),
            pltpu.SMEM((2,), jnp.int32),
            pltpu.SemaphoreType.DMA((2,)),
        ],
    )
    live = lax.ppermute(live, ("sec", "op"), crossing)
    left, right, shift = load(left_ops, right_ops, term_shift, field)
    got, left, right, live = lax.optimization_barrier((got, left, right, live))
    got = call(live_kernel, f32(block, block), [VMEM] * 2, got, live)
    send, *parts = product_to_send(
        shift, left, right, field, field_other, got, swapped(got), raw=True
    )
    total, peer = over_chips(product_to_keep(shift, left, right, *parts) + swapped(send))

    first = (total + peer) * mask
    one = lax.ppermute(first, ("sec", "op"), crossing)
    two = lax.ppermute(first, ("sec", "op"), crossing_too)
    first_other = swapped(first)
    sums = call(tile_kernel, f32(EXTRA, block), [VMEM] * 4, first, first_other, field, field_other)

    def with_distant(sums, step):
        return sums + lax.ppermute(sums, "sec", [(s, s ^ step) for s in range(sectors)])

    step = sectors // 2
    while step > 2:
        sums = with_distant(sums, step)
        step //= 2
    two, sums = lax.optimization_barrier((two, sums))
    send, *parts = product_to_send(
        shift, left, right, first, first_other, one, swapped(one), two, swapped(two)
    )
    keep = product_to_keep(shift, left, right, *parts)
    sums = call(
        added_kernel,
        f32(EXTRA, block),
        [VMEM] * 3,
        sums, lax.ppermute(sums, "sec", [(s, s ^ 2) for s in range(sectors)]), keep,
        cost_estimate=pl.CostEstimate(flops=10**10, bytes_accessed=0, transcendentals=0),
    )
    total, peer = over_chips(
        call(added_after_kernel, f32(half, block), [VMEM] * 3, keep, swapped(send), sums)
    )

    pair_sums = lax.ppermute(sums, "sec", pairs)
    peer, pair_sums = lax.optimization_barrier((peer, pair_sums))
    cells = sectors * block * block
    merged = call(
        lambda *refs: merged_kernel(cells, *refs),
        f32(EXTRA, block),
        [VMEM] * 2,
        sums, pair_sums,
    )
    correction = call(
        correction_kernel,
        f32(1, block, block),
        [VMEM] * 5,
        merged, first, first_other, field, field_other,
    )
    image = call(
        image_kernel,
        f32(1, block, block),
        [VMEM] * 9,
        merged, total, peer, mask, first, swapped(total), swapped(peer), mask_other, first_other,
    )
    return correction, image


def solution(mesh):
    in_specs = (
        P("sec", None, None),
        P("op", "sec", None, None),
        P("op", "sec", None, None),
        P("op"),
        P("sec"),
        P("sec"),
    )
    out_specs = (P("sec", None, None), P("sec", None, None))
    return jax.shard_map(local, mesh=mesh, in_specs=in_specs, out_specs=out_specs, check_vma=False)
```

```python
import jax
import jax.numpy as jnp
from jax import lax
from jax.experimental import pallas as pl
from jax.experimental.pallas import tpu as pltpu
from jax.sharding import PartitionSpec as P

EXTRA = 8
VMEM = pl.BlockSpec(memory_space=pltpu.VMEM)
HBM = pl.BlockSpec(memory_space=pltpu.HBM)


def f32(*shape):
    return jax.ShapeDtypeStruct(shape, jnp.float32)


def in_hbm(x):
    return pltpu.with_memory_space_constraint(x, pltpu.HBM)


def call(kernel, out_shape, in_specs, *arrays, mib=4, **options):
    return pl.pallas_call(
        kernel,
        out_shape=out_shape,
        in_specs=in_specs,
        out_specs=jax.tree.map(lambda _: VMEM, out_shape),
        compiler_params=pltpu.CompilerParams(vmem_limit_bytes=mib * 1024 * 1024),
        **options,
    )(*arrays)


def core_index():
    return lax.rem(lax.axis_index("op"), 2)


def rows_of(core, half):
    return pl.ds(pl.multiple_of(core * half, half), half)


def split(x):
    high = x.astype(jnp.bfloat16)
    low = (x - high.astype(jnp.float32)).astype(jnp.bfloat16)
    return high, low


def dot(a, b):
    return jnp.dot(a, b, preferred_element_type=jnp.float32)


def total_of(x):
    return jnp.sum(jnp.sum(x, axis=0, keepdims=True), axis=1, keepdims=True)


def inside(shape, first_row, rows, cols):
    row = lax.broadcasted_iota(jnp.int32, shape, 0) + first_row
    return (row < rows) & (lax.broadcasted_iota(jnp.int32, shape, 1) < cols)


def field_kernel(state_ref, live_ref, field_ref, other_ref, mask_ref, live_out, state, live, sems):
    copies = [
        pltpu.make_async_copy(ref, buffer, sems.at[i])
        for i, (ref, buffer) in enumerate(((state_ref, state), (live_ref, live)))
    ]
    for copy in copies:
        copy.start()
    for copy in copies:
        copy.wait()
    half = mask_ref.shape[0]
    core = core_index()
    rows, cols = live[0], live[1]
    for which, ref in ((core, field_ref), (1 - core, other_ref)):
        start = which * half
        ref[...] = jnp.where(inside(ref.shape, start, rows, cols), state[0, rows_of(which, half)], 0.0)
    mask_ref[...] = jnp.where(inside(mask_ref.shape, core * half, rows, cols), 1.0, 0.0)
    row = lax.broadcasted_iota(jnp.int32, live_out.shape, 0)
    live_out[...] = jnp.where(row == 0, rows, cols)


def load_kernel(left_ref, right_ref, shift_ref, field_ref, left_out, right_out, shift_out, right, shift, sems):
    terms = left_ref.shape[0]
    shifts = pltpu.make_async_copy(shift_ref, shift, sems.at[2, 0])
    rights = [
        pltpu.make_async_copy(right_ref.at[term], right.at[term], sems.at[0, term])
        for term in range(terms)
    ]
    lefts = [
        pltpu.make_async_copy(left_ref.at[term], left_out.at[term], sems.at[1, term])
        for term in range(terms)
    ]
    for copy in (shifts, *rights, *lefts):
        copy.start()
    shifts.wait()
    for term in range(terms):
        shift_out[term] = jnp.full(shift_out.shape[1:], shift[term], jnp.int32)
    for term in range(terms):
        rights[term].wait()
        right_out[term, 0] = right[term, 0].T
    for copy in lefts:
        copy.wait()


def load(left_ops, right_ops, shift, field):
    terms = shift.shape[0]
    return call(
        load_kernel,
        [f32(*left_ops.shape), f32(*right_ops.shape), jax.ShapeDtypeStruct((terms, 8, 128), jnp.int32)],
        [HBM, HBM, HBM, VMEM],
        in_hbm(left_ops), in_hbm(right_ops), in_hbm(shift), field,
        mib=8,
        scratch_shapes=[
            pltpu.VMEM(right_ops.shape, jnp.float32),
            pltpu.SMEM(shift.shape, jnp.int32),
            pltpu.SemaphoreType.DMA((3, terms)),
        ],
        cost_estimate=pl.CostEstimate(flops=0, bytes_accessed=8 * left_ops.size, transcendentals=0),
    )


def half_product(which, shift_ref, high, low, left_ref, right_ref):
    half = left_ref.shape[2] // 2
    rows = rows_of(which, half)

    def thrice(a, b):
        (a_high, a_low), (b_high, b_low) = a, b
        both = dot(jnp.concatenate([a_high, a_low]), b_high)
        return both[:half] + (both[half:] + dot(a_high, b_low))

    inner = []
    for term in range(left_ref.shape[0]):
        source = 1 - shift_ref[term][0, 0]
        inner.append(thrice(split(left_ref[term, 0, rows]), (high[source], low[source])))
    out = None
    for term in range(right_ref.shape[0]):
        part = thrice(split(inner[term]), split(right_ref[term, 0]))
        out = part if out is None else out + part
    return out


def send_kernel(raw, shift_ref, left_ref, right_ref, own_ref, own_other_ref, *refs):
    *refs, send_ref, high, low = refs
    half, block = send_ref.shape
    core, sector = core_index(), lax.axis_index("sec")
    slot = jnp.where(lax.rem(sector, 2) == 0, 2, 0)
    got = jnp.where(core == 1, slot, 2 - slot)

    def put(index, mine_ref, other_ref):
        for which, ref in ((core, mine_ref), (1 - core, other_ref)):
            rows = rows_of(which, half)
            high[index, rows], low[index, rows] = split(ref[...])

    put(1, own_ref, own_other_ref)
    if raw:
        for index, ref, live_ref in zip((got, 2 - got), refs[:2], refs[2:]):
            live = inside((block, block), 0, live_ref[:1, :1], live_ref[1:2, :1])
            high[index], low[index] = split(jnp.where(live, ref[...], 0.0))
    else:
        one_ref, one_other_ref, two_ref, two_other_ref = refs
        put(got, one_ref, two_other_ref)
        put(2 - got, two_ref, one_other_ref)

    @pl.when(sector == 0)
    def _():
        high[0] = jnp.zeros(high.shape[1:], high.dtype)
        low[0] = jnp.zeros(low.shape[1:], low.dtype)

    @pl.when(sector == lax.axis_size("sec") - 1)
    def _():
        high[2] = jnp.zeros(high.shape[1:], high.dtype)
        low[2] = jnp.zeros(low.shape[1:], low.dtype)

    send_ref[...] = half_product(1 - core, shift_ref, high, low, left_ref, right_ref)


def keep_kernel(shift_ref, left_ref, right_ref, high, low, *refs):
    refs[-1][...] = half_product(core_index(), shift_ref, high, low, left_ref, right_ref)


def product_options(left, count=30):
    terms, _, block, _ = left.shape
    return dict(
        mib=16,
        cost_estimate=pl.CostEstimate(
            flops=count * terms * block**3, bytes_accessed=8 * left.size, transcendentals=0
        ),
    )


def product_to_send(shift, left, right, *arrays, raw=False):
    block = left.shape[-1]
    arrays = [shift, left, right, *arrays]
    return call(
        lambda *refs: send_kernel(raw, *refs),
        [f32(block // 2, block)] + [jax.ShapeDtypeStruct((3, block, block), jnp.bfloat16)] * 2,
        [VMEM] * len(arrays),
        *arrays,
        **product_options(left),
    )


def product_to_keep(shift, left, right, high, low, *after):
    block = left.shape[-1]
    arrays = [shift, left, right, high, low, *after]
    return call(
        keep_kernel, f32(block // 2, block), [VMEM] * len(arrays), *arrays, **product_options(left, 1)
    )


def tile_kernel(first_ref, first_other_ref, field_ref, field_other_ref, out_ref):
    first = jnp.concatenate([first_ref[...], first_other_ref[...]])
    field = jnp.concatenate([field_ref[...], field_other_ref[...]])
    cross, square = total_of(field * first), total_of(field * field)
    theta = jnp.where(square > 0, cross / jnp.where(square > 0, square, 1.0), 0.0)
    resid = first - theta * field
    energy = total_of(resid * resid)
    row = lax.broadcasted_iota(jnp.int32, out_ref.shape, 0)
    lane = lax.broadcasted_iota(jnp.int32, out_ref.shape, 1)
    values = jnp.where(row == 0, cross, jnp.where(row == 1, square, jnp.where(row == 2, energy, 0.0)))
    out_ref[...] = jnp.where(lane == lax.axis_index("sec"), values, 0.0)


def added_after_kernel(a_ref, b_ref, after_ref, out_ref):
    out_ref[...] = a_ref[...] + b_ref[...]


def added_kernel(a_ref, b_ref, after_ref, out_ref):
    out_ref[...] = a_ref[...] + b_ref[...]


def merged_kernel(cells, sums_ref, got_ref, out_ref):
    sums = sums_ref[...] + got_ref[...]
    crosses, squares, energies = (sums[i : i + 1] for i in range(3))
    theta = jnp.sum(crosses, axis=1, keepdims=True) / jnp.sum(squares, axis=1, keepdims=True)
    thetas = jnp.where(squares > 0, crosses / jnp.where(squares > 0, squares, 1.0), 0.0)
    energy = jnp.sum(energies + (thetas - theta) ** 2 * squares, axis=1, keepdims=True)
    scale = lax.rsqrt(energy / cells + 1e-06)
    row = lax.broadcasted_iota(jnp.int32, out_ref.shape, 0)
    out_ref[...] = jnp.where(row == 0, theta, scale)


def image_kernel(merged_ref, total_ref, peer_ref, mask_ref, first_ref, out_ref):
    theta, scale = merged_ref[0:1, :], merged_ref[1:2, :]
    total = (total_ref[...] + peer_ref[...]) * mask_ref[...]
    out_ref[...] = scale * (total - theta * first_ref[...])


def correction_kernel(merged_ref, first_ref, first_other_ref, field_ref, field_other_ref, out_ref):
    half = first_ref.shape[0]
    core = core_index()
    theta, scale = merged_ref[0:1, :], merged_ref[1:2, :]
    out_ref[0, rows_of(core, half)] = scale * (first_ref[...] - theta * field_ref[...])
    out_ref[0, rows_of(1 - core, half)] = scale * (first_other_ref[...] - theta * field_other_ref[...])


def output_kernel(mine_ref, other_ref, out_ref):
    half = mine_ref.shape[0]
    core = core_index()
    out_ref[0, rows_of(core, half)] = mine_ref[...]
    out_ref[0, rows_of(1 - core, half)] = other_ref[...]


def local(state, left_ops, right_ops, term_shift, sector_rows, sector_cols):
    sectors, ops = lax.axis_size("sec"), lax.axis_size("op")
    block = state.shape[1]
    half = block // 2

    others = [(i, i ^ 1) for i in range(ops)]
    pairs = [(s, s ^ 1) for s in range(sectors)]
    between = []
    for a in range(ops):
        between += [(s * ops + a, s * ops + (a ^ 2)) for s in (0, sectors - 1)]
        for s in range(1, sectors - 1, 2):
            between += [(s * ops + a, (s + 1) * ops + a), ((s + 1) * ops + a, s * ops + a)]

    def swapped(v):
        return lax.ppermute(v, "op", others)

    def over_chips(total):
        step = 2
        while step < ops // 2:
            total = total + lax.ppermute(total, "op", [(i, i ^ step) for i in range(ops)])
            step *= 2
        return total, lax.ppermute(total, "op", [(i, i ^ step) for i in range(ops)])

    crossing = [(s * ops + a, (s ^ 1) * ops + a) for s in range(sectors) for a in range(1, ops, 2)]
    crossing += [(source, target) for source, target in between if source % 2 == 0]
    crossing_too = [(s * ops + a, (s ^ 1) * ops + a) for s in range(sectors) for a in range(0, ops, 2)]
    crossing_too += [(source, target) for source, target in between if source % 2]
    got = lax.ppermute(state[0], ("sec", "op"), crossing)
    field, field_other, mask, live = call(
        field_kernel,
        [f32(half, block)] * 3 + [jax.ShapeDtypeStruct((8, 128), jnp.int32)],
        [HBM] * 2,
        in_hbm(state), jnp.concatenate([sector_rows, sector_cols]),
        scratch_shapes=[
            pltpu.VMEM((1, block, block), jnp.float32),
            pltpu.SMEM((2,), jnp.int32),
            pltpu.SemaphoreType.DMA((2,)),
        ],
    )
    live = lax.ppermute(live, ("sec", "op"), crossing)
    left, right, shift = load(left_ops, right_ops, term_shift, field)
    got, left, right, live = lax.optimization_barrier((got, left, right, live))
    send, *parts = product_to_send(
        shift, left, right, field, field_other, got, swapped(got), live, swapped(live), raw=True
    )
    total, peer = over_chips(product_to_keep(shift, left, right, *parts) + swapped(send))

    first = (total + peer) * mask
    one = lax.ppermute(first, ("sec", "op"), crossing)
    two = lax.ppermute(first, ("sec", "op"), crossing_too)
    first_other = swapped(first)
    sums = call(tile_kernel, f32(EXTRA, block), [VMEM] * 4, first, first_other, field, field_other)

    def with_distant(sums, step):
        return sums + lax.ppermute(sums, "sec", [(s, s ^ step) for s in range(sectors)])

    step = sectors // 2
    while step > 2:
        sums = with_distant(sums, step)
        step //= 2
    two, sums = lax.optimization_barrier((two, sums))
    send, *parts = product_to_send(
        shift, left, right, first, first_other, one, swapped(one), two, swapped(two)
    )
    keep = product_to_keep(shift, left, right, *parts)
    sums = call(
        added_kernel,
        f32(EXTRA, block),
        [VMEM] * 3,
        sums, lax.ppermute(sums, "sec", [(s, s ^ 2) for s in range(sectors)]), keep,
        cost_estimate=pl.CostEstimate(flops=10**10, bytes_accessed=0, transcendentals=0),
    )
    total, peer = over_chips(
        call(added_after_kernel, f32(half, block), [VMEM] * 3, keep, swapped(send), sums)
    )

    cells = sectors * block * block
    merged = call(
        lambda *refs: merged_kernel(cells, *refs),
        f32(EXTRA, block),
        [VMEM] * 2,
        sums, lax.ppermute(sums, "sec", pairs),
    )
    image = call(image_kernel, f32(half, block), [VMEM] * 5, merged, total, peer, mask, first)
    correction = call(
        correction_kernel,
        f32(1, block, block),
        [VMEM] * 5,
        merged, first, first_other, field, field_other,
    )
    image = call(output_kernel, f32(1, block, block), [VMEM] * 2, image, swapped(image))
    return correction, image


def solution(mesh):
    in_specs = (
        P("sec", None, None),
        P("op", "sec", None, None),
        P("op", "sec", None, None),
        P("op"),
        P("sec"),
        P("sec"),
    )
    out_specs = (P("sec", None, None), P("sec", None, None))
    return jax.shard_map(local, mesh=mesh, in_specs=in_specs, out_specs=out_specs, check_vma=False)
```
